512 devices in a mesh: gx: 32 (over x_lo, y, core), gy: 16 (over z, x_hi).
Axes of the slice: x: 4 (x_hi: 2, x_lo: 2; x = x_hi * 2 + x_lo), y: 8, z: 8, core: 2. Of those that a mesh axis runs over, the one named last changes fastest.
Arguments:
- charges: float32 [2, 786432], P(None, ('gx', 'gy')), may hold values from -6 to 6
- source_slot: int32 [786432], P(('gx', 'gy')), may hold values from 0 to 2047, as said below
- tile_anchor: int32 [8192, 3], P(('gx', 'gy')), may hold values from 0 to 511, as said below
- projection: bfloat16 [8192, 256, 128], P(('gx', 'gy')), may hold values from -0.5 to 0.5
- near_pairs: int32 [4096, 2], P(('gx', 'gy')), may hold values from 0 to 15
- near_blocks: bfloat16 [4096, 2, 128, 128], P(('gx', 'gy')), may hold values from -0.5 to 0.5
- green_real: float32 [512, 512, 32], P(None, 'gx', 'gy'), may hold values from -2 to 4
- green_imag: float32 [512, 512, 32], P(None, 'gx', 'gy'), may hold values from -12 to 12
Outputs:
- potential: float32 [2, 786432], P(None, ('gx', 'gy'))
The draws below stay inside these ranges and needn't reach their ends.
Inputs may be any that keep to these rules, and one draw needn't show every extreme that they name: `source_slot`: on each device the 1536 sources occupy distinct slots among the device's 16 tiles of 128 slots; the other slots are empty. `tile_anchor`: tile t belongs to device t // 16, devices in the order gx then gy; its anchor's first two coordinates lie in that device's block of 16 x 32 cells, the third between 0 and 28.
All inputs are finite; a program needn't handle non-finite values.
Results may differ from the reference program's by a relative error of at most 0.0036.
Values may be sent and summed in bfloat16 or wider, within the bound.
No kernel may reach another device: no remote copies, remote signals or barrier semaphores. Data moves between devices by JAX's collectives and lax.ppermute only.
A program may use at most 128 MiB of HBM per device.

```python
import jax
import jax.numpy as jnp
from jax import lax

NX = 512
NY = 512
NZ = 32
BOX = 8
BZ = 4
P_SIZE = 256
S = 128
TILES_DEV = 16
SRC_DEV = 1536
PAIRS_DEV = 8
TILES = 8192
SOURCES = 786432
PAIRS = 4096
CX = 16
CY = 32


def draw_source_slot(key, part):
    key = jax.random.fold_in(key, 11)
    keys = jax.random.split(key, SOURCES // SRC_DEV)
    picks = jax.vmap(lambda single: jax.random.permutation(single, TILES_DEV * S)[:SRC_DEV])(keys)
    return picks.reshape(-1).astype(jnp.int32)


def draw_tile_anchor(key, part):
    key = jax.random.fold_in(key, 23)
    key_x, key_y, key_z = jax.random.split(key, 3)
    tile = jnp.arange(TILES, dtype=jnp.int32)
    device = tile // TILES_DEV
    columns = NY // CY
    row_block = device // columns
    col_block = device % columns
    anchor_x = row_block * CX + jax.random.randint(key_x, (TILES,), 0, CX, dtype=jnp.int32)
    anchor_y = col_block * CY + jax.random.randint(key_y, (TILES,), 0, CY, dtype=jnp.int32)
    anchor_z = jax.random.randint(key_z, (TILES,), 0, NZ - BZ + 1, dtype=jnp.int32)
    anchor_x = anchor_x.at[0].set(0).at[TILES - 1].set(NX - 1)
    anchor_y = anchor_y.at[0].set(0).at[TILES - 1].set(NY - 1)
    anchor_z = anchor_z.at[0].set(0)
    return jnp.stack([anchor_x, anchor_y, anchor_z], axis=1).astype(jnp.int32)


def place_ends(drawn, rng, smallest, high):
    longest = drawn.shape.index(max(drawn.shape))
    spots = []
    for shift in (0, 1):
        where = [jax.random.randint(jax.random.fold_in(rng, axis), (), 0, length) for axis, length in enumerate(drawn.shape)]
        where[longest] = (where[longest] + shift) % drawn.shape[longest]
        spots.append(tuple(where))
    return drawn.at[spots[0]].set(smallest).at[spots[1]].set(high)


def shard_levels(stream_key, shape, pieces, smallest, largest):
    def one(axis_at, shards_of):
        draws = jax.random.uniform(jax.random.fold_in(jax.random.fold_in(stream_key, 6), axis_at), (shards_of,), jnp.float32, smallest / len(pieces), largest / len(pieces))
        return jnp.repeat(jnp.exp(draws), shape[axis_at] // shards_of).reshape((-1,) + (1,) * (len(shape) - axis_at - 1))

    level = one(*pieces[0])
    for cut in pieces[1:]:
        level = level * one(*cut)
    return level


def bell_draw(own_key, shape, scale, limit, shards=(), kind=jnp.bfloat16):
    drawn = jax.random.normal(own_key, shape, jnp.float32) * scale
    if len(shards) > 0:
        drawn = shard_levels(own_key, shape, shards, -0.22, 0.18) * drawn
    return jnp.clip(drawn, min=-limit, max=limit).astype(kind)


def setup_inputs(seed: int = 0) -> dict:
    key_list = jax.random.split(jax.random.key(seed), 9)
    charges = bell_draw(key_list[0], (2, SOURCES), 1.0, 6.0, ((1, 512),), jnp.float32)
    source_slot = draw_source_slot(jax.random.fold_in(key_list[8], 71), 0)
    tile_anchor = draw_tile_anchor(jax.random.fold_in(key_list[8], 71), 0)
    projection = bell_draw(key_list[3], (TILES, P_SIZE, S), S ** -0.5, 0.5, ((0, 512),))
    near_pairs = place_ends(jax.random.randint(key_list[4], (PAIRS, 2), 0, TILES_DEV), jax.random.fold_in(key_list[4], 1), 0, TILES_DEV - 1).astype(jnp.int32)
    near_blocks = bell_draw(key_list[5], (PAIRS, 2, S, S), S ** -0.5, 0.5, ((0, 512),))
    green_real = jnp.clip(-2.0 + 6.0 * jax.random.uniform(key_list[6], (NX, NY, NZ), jnp.float32) ** shard_levels(key_list[6], (NX, NY, NZ), ((1, 32), (2, 16)), -0.2, 0.2), -2.0, 4.0)
    green_imag = bell_draw(key_list[7], (NX, NY, NZ), 2.0, 12.0, ((1, 32), (2, 16)), jnp.float32)
    return {"charges": charges, "source_slot": source_slot, "tile_anchor": tile_anchor, "projection": projection, "near_pairs": near_pairs, "near_blocks": near_blocks, "green_real": green_real, "green_imag": green_imag}


TOP_PRECISION = lax.Precision.HIGHEST


def node_index(tile_anchor):
    offsets = jnp.arange(BOX * BOX * BZ, dtype=jnp.int32)
    box_x = offsets // (BOX * BZ)
    box_y = (offsets // BZ) % BOX
    box_z = offsets % BZ
    reach = BOX // 2 - 1
    grid_x = (tile_anchor[:, 0:1] - reach + box_x[None, :]) % NX
    grid_y = (tile_anchor[:, 1:2] - reach + box_y[None, :]) % NY
    grid_z = tile_anchor[:, 2:3] + box_z[None, :]
    return ((grid_x * NY + grid_y) * NZ + grid_z).astype(jnp.int32)


def reference(charges, source_slot, tile_anchor, projection, near_pairs, near_blocks, green_real, green_imag):
    devices = TILES // TILES_DEV
    owner = (jnp.arange(SOURCES, dtype=jnp.int32) // SRC_DEV) * (TILES_DEV * S)
    slot = (owner + source_slot).astype(jnp.int32)
    slot_flat = jnp.zeros((2, TILES * S), jnp.bfloat16).at[:, slot].set(charges.astype(jnp.bfloat16))
    slot_charges = jnp.moveaxis(slot_flat.reshape(2, devices, TILES_DEV, S), 1, 0)
    proj_blocks = projection.reshape(devices, TILES_DEV, P_SIZE, S)

    def project(items):
        weights, cargo = items
        return jnp.einsum('tps,cts->ctp', weights.astype(jnp.float32), cargo.astype(jnp.float32), precision=TOP_PRECISION)

    node_values = lax.map(project, (proj_blocks, slot_charges))
    node_values = jnp.moveaxis(node_values, 0, 1).reshape(2, -1)
    index = node_index(tile_anchor).reshape(-1)
    grid = jnp.zeros((2, NX * NY * NZ), jnp.float32).at[:, index].add(node_values).reshape(2, NX, NY, NZ)
    spectrum = jnp.fft.fftn(lax.complex(grid[0], grid[1]))
    far = jnp.fft.ifftn(spectrum * lax.complex(green_real, green_imag))
    far = jnp.stack([jnp.real(far), jnp.imag(far)]).astype(jnp.bfloat16).reshape(2, -1)
    far_nodes = jnp.moveaxis(far[:, index].reshape(2, devices, TILES_DEV, P_SIZE), 1, 0)
    pair_blocks = near_pairs.reshape(devices, PAIRS_DEV, 2)
    block_split = near_blocks.reshape(devices, PAIRS_DEV, 2, S, S)

    def settle(items):
        weights, cargo, values, pairs, blocks = items
        far_part = jnp.einsum('tps,ctp->cts', weights.astype(jnp.float32), values.astype(jnp.float32), precision=TOP_PRECISION)
        source = cargo[:, pairs[:, 1]].astype(jnp.float32)
        mats = blocks.astype(jnp.float32)
        real_component = jnp.einsum('pab,pb->pa', mats[:, 0], source[0], precision=TOP_PRECISION) - jnp.einsum('pab,pb->pa', mats[:, 1], source[1], precision=TOP_PRECISION)
        imaginary_component = jnp.einsum('pab,pb->pa', mats[:, 0], source[1], precision=TOP_PRECISION) + jnp.einsum('pab,pb->pa', mats[:, 1], source[0], precision=TOP_PRECISION)
        match_count = (pairs[:, 0:1] == jnp.arange(TILES_DEV, dtype=jnp.int32)[None, :]).astype(jnp.float32)
        nearby_component = jnp.einsum('vk,evo->eko', match_count, jnp.stack([real_component, imaginary_component]), precision=TOP_PRECISION)
        return far_part + nearby_component

    total = lax.map(settle, (proj_blocks, slot_charges, far_nodes, pair_blocks, block_split))
    total = jnp.moveaxis(total, 0, 1).reshape(2, -1)
    return total[:, slot]
```

```python
import functools

import jax
import jax.numpy as jnp
import ml_dtypes
import numpy as np
from jax import lax
from jax.experimental import pallas as pl
from jax.experimental.pallas import tpu as pltpu
from jax.sharding import PartitionSpec as P

TILES = 16
SLOTS = 128
SOURCES = 1536
NU = 12
UPAD = 16
NV = 40
CELLS = 512
F32 = jnp.float32
BF16 = jnp.bfloat16
VMEM_LIMIT = 48 * 1024 * 1024


def split_table(table):
    high = table.astype(np.float32).astype(ml_dtypes.bfloat16)
    low = (table - high.astype(np.float64)).astype(np.float32).astype(ml_dtypes.bfloat16)
    return high, low


def as_real(theta, inverse):
    sign = -1.0 if inverse else 1.0
    cos, sin = np.cos(theta), sign * np.sin(theta)
    return np.stack([np.stack([cos, sin], -1), np.stack([-sin, cos], -1)], -2)


def z_tables():
    kz = np.arange(32)
    theta = 2.0 * np.pi * (np.outer(kz, kz) % 32) / 32
    forward = as_real(theta, False).reshape(16, 2, 32, 2, 2)
    table = np.einsum("jqzoc,hg->jhqogcz", forward, np.eye(2)).reshape(128, 128)
    backward = as_real(theta, True).reshape(16, 2, 32, 2, 2) / 32.0
    table_back = np.einsum("jqzoc,hg->jhqcgoz", backward, np.eye(2)).reshape(128, 128)
    return table, table_back


def y_tables():
    k = np.arange(16)
    theta = 2.0 * np.pi * (np.outer(k, k) % 16) / 16
    forward = as_real(theta, False)
    both = np.stack([forward, np.stack([forward[:, :, 1], -forward[:, :, 0]], 2)], 0)
    eyes = np.einsum("hg,qr->hgqr", np.eye(2), np.eye(2))
    table = np.einsum("nkjoc,hgqr->jhqcngokr", both, eyes).reshape(128, 256)
    backward = as_real(theta, True) / 512.0
    table_back = np.einsum("kjoc,hgqr->jgrohckq", backward, eyes).reshape(128, 128)
    phi = 2.0 * np.pi * np.outer(np.arange(NV) - 4, k) / 512
    wide = np.broadcast_to(phi[:, None, None, :, None], (NV, 2, 2, 16, 2)).reshape(NV, 128)
    turn = np.stack([np.cos(wide), np.sin(wide)]).astype(np.float32)
    psi = 2.0 * np.pi * (np.outer(np.arange(32), np.arange(NV) - 4) % 32) / 32
    rows = np.concatenate([np.cos(psi), np.sin(psi)], 1)
    rows_back = np.concatenate([np.cos(psi.T), -np.sin(psi.T)], 1)
    return table, table_back, turn, rows, rows_back


def x_tables():
    kx = np.arange(256)
    place = (8 * np.arange(32)[:, None] + np.arange(UPAD)[None, :] - 2).reshape(-1)
    real = np.broadcast_to((np.arange(UPAD) < NU)[None, :], (32, UPAD)).reshape(-1)
    theta = 2.0 * np.pi * (np.outer(kx, place) % 256) / 256
    cos, sin = np.cos(theta) * real, np.sin(theta) * real
    rows = np.concatenate([cos, sin], 0)
    rows_back = np.concatenate([cos.T, -sin.T], 1) / 512.0
    phi = 2.0 * np.pi * kx[:, None] * np.array([0.0, 1.0])[None, :] / 512
    wide = np.repeat(phi, 64, axis=1)
    turn = np.stack([np.cos(wide), np.sin(wide)]).astype(np.float32)
    return rows, rows_back, turn


def spread_table():
    p = np.arange(256)
    lane = (p // 32 % 2) * 128 + (p // 64) * NV + p // 4 % 8
    return (lane[:, None] == np.arange(256)[None, :]).astype(ml_dtypes.bfloat16)


def mm(a, b):
    return lax.dot_general(a, b, (((1,), (0,)), ((), ())), preferred_element_type=F32)


def mm_nt(a, b):
    return lax.dot_general(a, b, (((1,), (1,)), ((), ())), preferred_element_type=F32)


def halves(value):
    high = value.astype(BF16)
    return high, (value - high.astype(F32)).astype(BF16)


def iota(shape, axis):
    return lax.broadcasted_iota(jnp.int32, shape, axis)


def turned(value):
    bit = (iota(value.shape, 1) // 32) % 2
    return jnp.where(bit == 0, pltpu.roll(value, 96, 1), -pltpu.roll(value, 32, 1))


def crossed(value):
    half = iota(value.shape, 1) // 64
    return pltpu.roll(value, 64, 1) + jnp.where(half == 0, value, -value)


def z_places(anchor_ref, shape, axis):
    at = iota(shape, axis)
    tile = (at // 8) % TILES
    z = at % 4
    for t in range(TILES):
        z = z + jnp.where(tile == t, anchor_ref[t, 2], 0)
    return z


def layer_picks(anchor_ref):
    shape = (128, 256)
    z = z_places(anchor_ref, shape, 1)
    row, col = iota(shape, 0), iota(shape, 1)
    want = (col // 128) * 64 + ((col // 4) % 2) * 32 + z
    return jnp.where(row == want, 1.0, 0.0).astype(BF16)


def place(anchor_ref, t):
    x = (anchor_ref[t, 0] & 15) + 1
    y = (anchor_ref[t, 1] & 31) + 1
    starts = (((x + 1) >> 1) * NV + y, (x >> 1) * NV + y)
    return x & 1, starts


def spread_kernel(
    charges_ref, slot_ref, anchor_ref, proj_ref, tab_ref, spread_ref, out_ref, slots_ref, nodes, patch, cells
):
    slot = slot_ref[...]
    pick = jnp.where(iota((SLOTS, SOURCES), 0) == (slot & 127), 1.0, 0.0).astype(BF16)
    row = iota((128, SOURCES), 0)
    charge = jnp.where(row % 8 < 4, charges_ref[0:1, :], charges_ref[1:2, :])
    held = jnp.where(row // 8 == (slot >> 7), charge, 0.0).astype(BF16)
    slots_ref[...] = mm_nt(held, pick)
    for t in range(TILES):
        mine = slots_ref[8 * t : 8 * t + 8, :].astype(BF16)
        nodes[8 * t : 8 * t + 8, :] = mm_nt(mine, proj_ref[t])
    layer = iota((128, 256), 1) % 4 == iota((128, 256), 0) % 4
    high, low = halves(jnp.where(layer, nodes[...], 0.0))
    patch[...] = mm(high, spread_ref[...]) + mm(low, spread_ref[...])
    cells[...] = jnp.zeros_like(cells)
    empty = jnp.zeros((8, 128), F32)
    for t in range(TILES):
        odd, starts = place(anchor_ref, t)
        even_part = patch[8 * t : 8 * t + 8, 0:128]
        odd_part = patch[8 * t : 8 * t + 8, 128:256]
        parts = (jnp.where(odd == 1, odd_part, even_part), jnp.where(odd == 1, even_part, odd_part))
        for h in range(2):
            wide = jnp.concatenate([parts[h], empty], axis=1)
            wide = pltpu.roll(wide, starts[h] & 127, 1)
            lane = pl.multiple_of((starts[h] >> 7) * 128, 128)
            cells[128 * h + 8 * t : 128 * h + 8 * t + 8, pl.ds(lane, 256)] = wide
    picks = layer_picks(anchor_ref)
    phase_high = mm(tab_ref[0], picks).astype(BF16)
    phase_low = mm(tab_ref[1], picks).astype(BF16)
    high, low = halves(cells[...])
    out = mm(phase_high, high) + mm(phase_high, low) + mm(phase_low, high)
    out_ref[...] = out.astype(BF16)


def near_kernel(pairs_ref, slots_ref, blocks_ref, near_ref):
    near_ref[...] = jnp.zeros_like(near_ref)
    row = iota((8, 128), 0)
    for q in range(8):
        source = slots_ref[pl.ds(pl.multiple_of(pairs_ref[q, 1] * 8, 8), 8), :]
        other = pltpu.roll(source, 4, 0)
        plain = jnp.where(row % 4 == 0, source, 0.0).astype(BF16)
        turn = jnp.where(row == 0, -other, jnp.where(row == 4, other, 0.0)).astype(BF16)
        value = mm_nt(plain, blocks_ref[q, 0]) + mm_nt(turn, blocks_ref[q, 1])
        target = pl.ds(pl.multiple_of(pairs_ref[q, 0] * 8, 8), 8)
        near_ref[target, :] = near_ref[target, :] + value


def y_kernel(in_ref, tab_ref, turn_ref, rows_ref, out_ref, hold):
    data = in_ref[...].astype(F32).T.astype(BF16)
    both = mm(data, tab_ref[0]) + mm(data, tab_ref[1])
    cos, sin = turn_ref[0], turn_ref[1]
    hold[...] = jnp.zeros_like(hold)
    for u in range(NU):
        plain = both[NV * u : NV * (u + 1), 0:128]
        turn = both[NV * u : NV * (u + 1), 128:256]
        lines = jnp.concatenate([plain * cos + turn * sin, turn * cos - plain * sin], axis=0)
        high, low = halves(lines)
        out = mm(rows_ref[0], high) + mm(rows_ref[0], low) + mm(rows_ref[1], high)
        hold[pl.ds(u, 32, stride=UPAD), :] = out
    out_ref[...] = hold[...].astype(BF16)


def x_kernel(in_ref, real_ref, imag_ref, rows_ref, back_ref, turn_ref, out_ref):
    data = in_ref[...]
    both = mm(rows_ref[0], data) + mm(rows_ref[1], data)
    cos, sin = turn_ref[0], turn_ref[1]
    value = both[0:256] + turned(both[256:512])
    value = value * cos + turned(value) * sin
    value = crossed(value)

    def wide(green):
        first, second = green[:, 0:256], green[:, 256:512]
        return jnp.concatenate([first, first, second, second], axis=0).T

    value = value * wide(real_ref[...]) - turned(value) * wide(imag_ref[...])
    value = crossed(value)
    value = value * cos - turned(value) * sin
    high, low = halves(jnp.concatenate([value, turned(value)], axis=0))
    out = mm(back_ref[0], high) + mm(back_ref[0], low) + mm(back_ref[1], high)
    out_ref[...] = out.astype(BF16)


def y_back_kernel(in_ref, tab_ref, turn_ref, rows_ref, out_ref, hold, hold_turned):
    data = in_ref[...].astype(F32)
    hold[...] = data
    hold_turned[...] = turned(data)
    cos, sin = turn_ref[0], turn_ref[1]
    lines = []
    for u in range(NU):
        plain = hold[pl.ds(u, 32, stride=UPAD), :]
        turn = hold_turned[pl.ds(u, 32, stride=UPAD), :]
        four = jnp.concatenate(
            [jnp.concatenate([plain, turn], axis=1), jnp.concatenate([turn, -plain], axis=1)], axis=0
        ).astype(BF16)
        both = mm(rows_ref[0], four) + mm(rows_ref[1], four)
        lines.append(both[:, 0:128] * cos - both[:, 128:256] * sin)
    lines.append(jnp.zeros((CELLS - NU * NV, 128), F32))
    high, low = halves(jnp.concatenate(lines, axis=0))
    out = mm_nt(tab_ref[0], high) + mm_nt(tab_ref[0], low) + mm_nt(tab_ref[1], high)
    out_ref[...] = out.astype(BF16)


def gather_kernel(
    in_ref, slot_ref, anchor_ref, proj_ref, near_ref, tab_ref, spread_ref, out_ref, cells, patch, total
):
    picks = layer_picks(anchor_ref)
    phase_high = mm(tab_ref[0], picks).T.astype(BF16)
    phase_low = mm(tab_ref[1], picks).T.astype(BF16)
    data = in_ref[...]
    field = mm(phase_high, data) + mm(phase_low, data)
    cells[...] = field.astype(BF16).astype(F32)
    for t in range(TILES):
        odd, starts = place(anchor_ref, t)
        parts = []
        for h in range(2):
            lane = pl.multiple_of((starts[h] >> 7) * 128, 128)
            wide = cells[128 * h + 8 * t : 128 * h + 8 * t + 8, pl.ds(lane, 256)]
            parts.append(pltpu.roll(wide, (256 - (starts[h] & 127)) & 255, 1)[:, 0:128])
        patch[8 * t : 8 * t + 8, 0:128] = jnp.where(odd == 1, parts[1], parts[0])
        patch[8 * t : 8 * t + 8, 128:256] = jnp.where(odd == 1, parts[0], parts[1])
    layer = iota((128, 256), 1) % 4 == iota((128, 256), 0) % 4
    patch[...] = jnp.where(layer, mm_nt(patch[...].astype(BF16), spread_ref[...]), 0.0)
    for t in range(TILES):
        mine = patch[8 * t : 8 * t + 8, :].astype(BF16)
        total[8 * t : 8 * t + 8, :] = mm(mine, proj_ref[t])
    high, low = halves(total[...] + near_ref[...])
    slot = slot_ref[...]
    pick = jnp.where(iota((SLOTS, SOURCES), 0) == (slot & 127), 1.0, 0.0).astype(BF16)
    value = mm(high, pick) + mm(low, pick)
    tile = iota((128, SOURCES), 0) // 8
    value = jnp.where(tile == (slot >> 7), value, 0.0).reshape(TILES, 8, SOURCES).sum(axis=0)
    out_ref[...] = jnp.concatenate(
        [value[0:4].sum(axis=0, keepdims=True), value[4:8].sum(axis=0, keepdims=True)], axis=0
    )


VM = pl.BlockSpec(memory_space=pltpu.VMEM)
SM = pl.BlockSpec(memory_space=pltpu.SMEM)


def call(kernel, outs, in_specs, scratch, flops, moved):
    return pl.pallas_call(
        kernel,
        out_shape=outs,
        in_specs=in_specs,
        out_specs=[VM] * len(outs),
        scratch_shapes=scratch,
        compiler_params=pltpu.CompilerParams(vmem_limit_bytes=VMEM_LIMIT),
        cost_estimate=pl.CostEstimate(flops=flops, bytes_accessed=moved, transcendentals=0),
    )


def shape(*dims, dtype=F32):
    return jax.ShapeDtypeStruct(dims, dtype)


def swap(cells, axis, rows):
    parts = lax.axis_size(axis)
    moved = lax.all_to_all(cells.reshape(parts, rows, -1), axis, 0, 0, tiled=True)
    return moved.reshape(parts * rows, -1)


def pair(table):
    return jnp.asarray(np.stack(split_table(table)))


def body(charges, source_slot, tile_anchor, projection, near_pairs, near_blocks, green_real, green_imag):
    z_tab, z_back = z_tables()
    y_tab, y_back, y_turn, y_rows, y_rows_back = y_tables()
    x_rows, x_back, x_turn = x_tables()
    spread = jnp.asarray(spread_table())
    slot = source_slot.reshape(1, SOURCES)

    cells, slots = call(
        spread_kernel,
        [shape(128, CELLS, dtype=BF16), shape(128, SLOTS)],
        [VM, VM, SM, VM, VM, VM],
        [pltpu.VMEM((128, 256), F32), pltpu.VMEM((128, 256), F32), pltpu.VMEM((256, CELLS), F32)],
        10**9,
        2 * 10**6,
    )(charges, slot, tile_anchor, projection, pair(z_tab), spread)

    lines = swap(cells, "gy", 8)
    near = call(near_kernel, [shape(128, SLOTS)], [SM, VM, VM], [], 10**8, 10**6)(near_pairs, slots, near_blocks)[0]
    lines = call(
        y_kernel,
        [shape(512, 128, dtype=BF16)],
        [VM] * 4,
        [pltpu.VMEM((512, 128), F32)],
        10**8,
        10**6,
    )(lines, pair(y_tab), jnp.asarray(y_turn), pair(y_rows))[0]
    lines = swap(lines, "gx", UPAD)
    lines = call(x_kernel, [shape(512, 128, dtype=BF16)], [VM] * 6, [], 10**9, 2 * 10**6)(
        lines,
        green_real.transpose(1, 2, 0).reshape(32, 512),
        green_imag.transpose(1, 2, 0).reshape(32, 512),
        pair(x_rows),
        pair(x_back),
        jnp.asarray(x_turn),
    )[0]
    lines = swap(lines, "gx", UPAD)
    cells = call(
        y_back_kernel,
        [shape(128, CELLS, dtype=BF16)],
        [VM] * 4,
        [pltpu.VMEM((512, 128), F32)] * 2,
        10**8,
        10**6,
    )(lines, pair(y_back), jnp.asarray(y_turn), pair(y_rows_back))[0]
    cells = swap(cells, "gy", 8)
    return call(
        gather_kernel,
        [shape(2, SOURCES)],
        [VM, VM, SM, VM, VM, VM, VM],
        [pltpu.VMEM((256, CELLS), F32), pltpu.VMEM((128, 256), F32), pltpu.VMEM((128, SLOTS), F32)],
        10**9,
        2 * 10**6,
    )(cells, slot, tile_anchor, projection, near, pair(z_back), spread)[0]


def solution(mesh):
    return jax.shard_map(
        body,
        mesh=mesh,
        in_specs=(
            P(None, ("gx", "gy")),
            P(("gx", "gy")),
            P(("gx", "gy"), None),
            P(("gx", "gy"), None, None),
            P(("gx", "gy"), None),
            P(("gx", "gy"), None, None, None),
            P(None, "gx", "gy"),
            P(None, "gx", "gy"),
        ),
        out_specs=P(None, ("gx", "gy")),
        check_vma=False,
    )
```

```python
import math

import jax
import jax.numpy as jnp
import ml_dtypes
import numpy as np
from jax import lax
from jax.experimental import pallas as pl
from jax.experimental.pallas import tpu as pltpu
from jax.sharding import PartitionSpec as P

TILES = 16
SLOTS = 128
PAIRS = 8
SOURCES = 1536
NU = 12
UPAD = 16
NV = 40
CELLS = 512
F32 = jnp.float32
BF16 = jnp.bfloat16
VMEM_LIMIT = 16 * 1024 * 1024
LIMIT_A = 65536 * 1024 - 960 * 1024


def split_table(table):
    high = table.astype(np.float32).astype(ml_dtypes.bfloat16)
    low = (table - high.astype(np.float64)).astype(np.float32).astype(ml_dtypes.bfloat16)
    return high, low


def as_real(theta, inverse):
    sign = -1.0 if inverse else 1.0
    cos, sin = np.cos(theta), sign * np.sin(theta)
    return np.stack([np.stack([cos, sin], -1), np.stack([-sin, cos], -1)], -2)


def z_tables():
    kz = np.arange(32)
    theta = 2.0 * np.pi * (np.outer(kz, kz) % 32) / 32
    forward = as_real(theta, False).reshape(16, 2, 32, 2, 2)
    table = np.einsum("jqzoc,hg->jhqogcz", forward, np.eye(2)).reshape(128, 128)
    backward = as_real(theta, True).reshape(16, 2, 32, 2, 2) / 32.0
    table_back = np.einsum("jqzoc,hg->jhqcgoz", backward, np.eye(2)).reshape(128, 128)
    first = np.zeros((4096, 256), ml_dtypes.bfloat16)
    p = np.arange(256)
    first[p, (p // 32 % 2) * 128 + (p // 64) * NV + p // 4 % 8] = 1.0
    first[256:384, 0:128], first[256:384, 128:256] = split_table(table)
    return jnp.asarray(first), in_rows(table_back)


def in_rows(*tables):
    padded = [np.pad(table, ((0, 0), (0, 128 - table.shape[1]))) for table in tables]
    return jnp.asarray(np.concatenate(padded, 0).astype(np.float32))


def y_tables():
    k = np.arange(16)
    theta = 2.0 * np.pi * (np.outer(k, k) % 16) / 16
    eyes = np.einsum("hg,qr->hgqr", np.eye(2), np.eye(2))
    table = np.einsum("kjoc,hgqr->jhqcgokr", as_real(theta, False), eyes).reshape(128, 128)
    table_back = np.einsum("kjoc,hgqr->jgrohckq", as_real(theta, True) / 512.0, eyes).reshape(128, 128)
    phi = 2.0 * np.pi * np.outer(np.arange(NV) - 4, k) / 512
    wide = np.broadcast_to(phi[:, None, None, :, None], (NV, 2, 2, 16, 2)).reshape(NV, 128)
    psi = 2.0 * np.pi * (np.outer(np.arange(32), np.arange(NV) - 4) % 32) / 32
    rows = np.concatenate([np.cos(psi), np.sin(psi)], 1)
    rows_back = np.concatenate([np.cos(psi.T), -np.sin(psi.T)], 1)
    turn = (np.cos(wide), np.sin(wide))
    return in_rows(*turn, table, rows), in_rows(*turn, table_back, rows_back)


def x_tables():
    k0 = np.arange(32)
    alpha = 2.0 * np.pi * (np.outer(k0, k0) % 32) / 32
    rows = np.concatenate([np.cos(alpha), np.sin(alpha)], 1)
    rows_back = np.concatenate([np.cos(alpha), -np.sin(alpha)], 1) / 512.0
    beta = 2.0 * np.pi * np.outer(k0, np.arange(NU) - 2) / 256
    phi = 2.0 * np.pi * (k0[:, None] + 32 * np.arange(8)[None, :]) / 512
    return in_rows(rows, rows_back, np.concatenate([np.cos(beta), np.sin(beta), np.cos(phi), np.sin(phi)], 1))


def mm(a, b):
    return lax.dot_general(a, b, (((1,), (0,)), ((), ())), preferred_element_type=F32)


def mm_nt(a, b):
    return lax.dot_general(a, b, (((1,), (1,)), ((), ())), preferred_element_type=F32)


def halves(value):
    high = value.astype(BF16)
    return high, (value - high.astype(F32)).astype(BF16)


def iota(shape, axis):
    return lax.broadcasted_iota(jnp.int32, shape, axis)


def turned(value):
    bit = (iota(value.shape, 1) // 32) % 2
    return jnp.where(bit == 0, pltpu.roll(value, 96, 1), -pltpu.roll(value, 32, 1))


def crossed(value):
    half = iota(value.shape, 1) // 64
    return pltpu.roll(value, 64, 1) + jnp.where(half == 0, value, -value)


def layer_picks(anchor):
    fan = jnp.where(iota((TILES, 256), 0) == (iota((TILES, 256), 1) // 8) % TILES, 1.0, 0.0).astype(BF16)
    low = mm(anchor[2:3, :].astype(F32).astype(BF16), fan)
    at = iota((1, 256), 1)
    want = low + ((at // 128) * 64 + ((at // 4) % 2) * 32 + at % 4).astype(F32)
    return jnp.where(iota((128, 256), 0) == want.astype(jnp.int32), 1.0, 0.0).astype(BF16)


def place(anchor_ref, t):
    x = (anchor_ref[0, t] & 15) + 1
    y = (anchor_ref[1, t] & 31) + 1
    starts = (((x + 1) >> 1) * NV + y, (x >> 1) * NV + y)
    return x & 1, starts


def as_row(slot):
    return jnp.concatenate([slot[r : r + 1, :] for r in range(SOURCES // 128)], axis=1)


def slot_picks(slot):
    return jnp.where(iota((SLOTS, SOURCES), 0) == (slot & 127), 1.0, 0.0).astype(BF16)


def spread_kernel(
    charges_hbm,
    slot_hbm,
    anchor_hbm,
    pairs_hbm,
    proj_hbm,
    tables_hbm,
    out_ref,
    slots_ref,
    ints_ref,
    charges_ref,
    slot_ref,
    anchor_ref,
    anchor_vec,
    pairs_vec,
    proj_ref,
    tables_ref,
    nodes,
    layers,
    patch,
    cells,
    sems,
):
    fetched = (
        (charges_hbm, charges_ref),
        (slot_hbm, slot_ref),
        (anchor_hbm, anchor_ref),
        (anchor_hbm, anchor_vec),
        (pairs_hbm, pairs_vec),
        (proj_hbm, proj_ref),
        (tables_hbm.at[0:384], tables_ref),
    )
    copies = [pltpu.make_async_copy(src, dst, sems.at[n]) for n, (src, dst) in enumerate(fetched)]
    for copy in copies:
        copy.start()
    cells[...] = jnp.zeros_like(cells)
    for copy in copies[:5]:
        copy.wait()
    ints_ref[...] = jnp.zeros_like(ints_ref)
    ints_ref[0 : SOURCES // 128, :] = slot_ref[...]
    ints_ref[16:19, 0:TILES] = anchor_vec[...]
    ints_ref[20:22, 0:PAIRS] = pairs_vec[...]
    slot = as_row(slot_ref[...])
    row = iota((32, SOURCES), 0)
    charge = jnp.where(row % 2 == 0, charges_ref[0:1, :], charges_ref[1:2, :])
    held = jnp.where(row // 2 == (slot >> 7), charge, 0.0).astype(BF16)
    slots_ref[...] = mm_nt(held, slot_picks(slot))
    picks = layer_picks(anchor_vec[...])
    copies[5].wait()
    for t in range(TILES):
        nodes[2 * t : 2 * t + 2, :] = mm_nt(slots_ref[2 * t : 2 * t + 2, :].astype(BF16), proj_ref[t])
    value = nodes[...]
    layer = iota((32, 128), 1) % 4
    for half in range(2):
        for b in range(4):
            part = value[:, 128 * half : 128 * half + 128]
            layers[pl.ds(128 * half + b, 32, stride=4), :] = jnp.where(layer == b, part, 0.0)
    high, low = halves(jnp.concatenate([layers[0:128, :], layers[128:256, :]], axis=1))
    copies[6].wait()
    spread = tables_ref[0:256, :]
    patch[...] = mm(high, spread) + mm(low, spread)
    empty = jnp.zeros((8, 128), F32)
    for t in range(TILES):
        odd, starts = place(anchor_ref, t)
        even_part = patch[8 * t : 8 * t + 8, 0:128]
        odd_part = patch[8 * t : 8 * t + 8, 128:256]
        parts = (jnp.where(odd == 1, odd_part, even_part), jnp.where(odd == 1, even_part, odd_part))
        for h in range(2):
            wide = jnp.concatenate([parts[h], empty], axis=1)
            wide = pltpu.roll(wide, starts[h] & 127, 1)
            lane = pl.multiple_of((starts[h] >> 7) * 128, 128)
            cells[128 * h + 8 * t : 128 * h + 8 * t + 8, pl.ds(lane, 256)] = wide
    phase_high = mm(tables_ref[256:384, 0:128], picks).astype(BF16)
    phase_low = mm(tables_ref[256:384, 128:256], picks).astype(BF16)
    high, low = halves(cells[...])
    out = mm(phase_high, high) + mm(phase_high, low) + mm(phase_low, high)
    out_ref[...] = out.astype(BF16)


def y_kernel(in_ref, table_ref, out_ref, hold):
    data = in_ref[...].astype(F32).T.astype(BF16)
    cos, sin = table_ref[0:NV, :], table_ref[NV : 2 * NV, :]
    table = table_ref[2 * NV : 2 * NV + 128, :]
    high, low = halves(jnp.concatenate([table, turned(table)], axis=1))
    both = mm(data, high) + mm(data, low)
    rows = halves(table_ref[2 * NV + 128 : 2 * NV + 160, 0 : 2 * NV])
    hold[...] = jnp.zeros_like(hold)
    for u in range(NU):
        plain = both[NV * u : NV * (u + 1), 0:128]
        turn = both[NV * u : NV * (u + 1), 128:256]
        lines = jnp.concatenate([plain * cos + turn * sin, turn * cos - plain * sin], axis=0)
        high, low = halves(lines)
        out = mm(rows[0], high) + mm(rows[0], low) + mm(rows[1], high)
        hold[pl.ds(u, 32, stride=UPAD), :] = out
    out_ref[...] = hold[...].astype(BF16)


def rotated(value, cos, sin):
    plain, turn = value
    return plain * cos + turn * sin, turn * cos - plain * sin


def eighths(value, count, sign):
    plain, turn = value
    if count == 0:
        return value
    if count == 2:
        return (turn, -plain) if sign > 0 else (-turn, plain)
    if count == 3:
        return eighths(eighths(value, 2, sign), 1, sign)
    root = math.sqrt(0.5)
    if sign > 0:
        return (plain + turn) * root, (turn - plain) * root
    return (plain - turn) * root, (turn + plain) * root


def short_dft(values, sign):
    count = len(values)
    if count == 1:
        return values
    even, odd = short_dft(values[0::2], sign), short_dft(values[1::2], sign)
    odd = [eighths(value, 8 // count * n, sign) for n, value in enumerate(odd)]
    sums = [(a[0] + b[0], a[1] + b[1]) for a, b in zip(even, odd)]
    return sums + [(a[0] - b[0], a[1] - b[1]) for a, b in zip(even, odd)]


def line_pair(rows, plain, turn):
    four = jnp.concatenate(
        [jnp.concatenate([plain, turn], axis=1), jnp.concatenate([turn, -plain], axis=1)], axis=0
    ).astype(BF16)
    return mm(rows[0], four) + mm(rows[1], four)


def x_kernel(in_ref, real_ref, imag_ref, table_ref, out_ref, hold, hold_turned):
    into = halves(table_ref[0:32, 0:64])
    back = halves(table_ref[32:64, 0:64])
    angles = table_ref[64:96, :]
    second = iota((32, 128), 1) >= 64

    def step(u):
        shape = (32, 128)
        cos, sin = angles[:, u : u + 1], angles[:, NU + u : NU + u + 1]
        return jnp.broadcast_to(cos, shape), jnp.broadcast_to(sin, shape)

    def fold(n):
        n = n + 2 * NU
        return jnp.where(second, angles[:, n : n + 1], 1.0), jnp.where(second, angles[:, n + 8 : n + 9], 0.0)

    data = in_ref[...].astype(F32)
    hold[...] = data
    hold_turned[...] = turned(data)
    classes = [None] * 8
    for u in range(NU):
        plain = hold[pl.ds(u, 32, stride=UPAD), :]
        both = line_pair(into, plain, hold_turned[pl.ds(u, 32, stride=UPAD), :])
        value = rotated((both[:, 0:128], both[:, 128:256]), *step(u))
        at = (u - 2) % 8
        classes[at] = value if classes[at] is None else tuple(a + b for a, b in zip(classes[at], value))
    lines = short_dft(classes, 1)

    def wide(green):
        green = green.reshape(32, 512)
        first, second = green[:, 0:256], green[:, 256:512]
        return jnp.concatenate([first, first, second, second], axis=0).T

    real, imag = wide(real_ref[...]), wide(imag_ref[...])
    for n in range(8):
        rows = slice(32 * n, 32 * n + 32)
        cos, sin = fold(n)
        plain, turn = rotated(lines[n], cos, sin)
        plain, turn = crossed(plain), crossed(turn)
        plain, turn = plain * real[rows] - turn * imag[rows], turn * real[rows] + plain * imag[rows]
        lines[n] = rotated((crossed(plain), crossed(turn)), cos, -sin)
    classes = short_dft(lines, -1)
    for u in range(NU):
        cos, sin = step(u)
        value = rotated(classes[(u - 2) % 8], cos, -sin)
        high, low = halves(jnp.concatenate(value, axis=0))
        out = mm(back[0], high) + mm(back[0], low) + mm(back[1], high)
        hold[pl.ds(u, 32, stride=UPAD), :] = out
    out_ref[...] = hold[...].astype(BF16)


def y_back_kernel(in_ref, table_ref, out_ref, hold, hold_turned):
    data = in_ref[...].astype(F32)
    hold[...] = data
    hold_turned[...] = turned(data)
    cos, sin = table_ref[0:NV, :], table_ref[NV : 2 * NV, :]
    tab = halves(table_ref[2 * NV : 2 * NV + 128, :])
    rows = halves(table_ref[2 * NV + 128 : 3 * NV + 128, 0:64])
    lines = []
    for u in range(NU):
        plain = hold[pl.ds(u, 32, stride=UPAD), :]
        turn = hold_turned[pl.ds(u, 32, stride=UPAD), :]
        both = line_pair(rows, plain, turn)
        lines.append(both[:, 0:128] * cos - both[:, 128:256] * sin)
    lines.append(jnp.zeros((CELLS - NU * NV, 128), F32))
    high, low = halves(jnp.concatenate(lines, axis=0))
    out = mm_nt(tab[0], high) + mm_nt(tab[0], low) + mm_nt(tab[1], high)
    out_ref[...] = out.astype(BF16)


def node_lanes():
    node = iota((256, 256), 0)
    lane = ((node >> 5) & 1) * 128 + (node >> 6) * NV + ((node >> 2) & 7)
    return jnp.where(iota((256, 256), 1) == lane, 1.0, 0.0).astype(BF16)


def gather_kernel(
    in_ref,
    ints_ref,
    proj_ref,
    slots_ref,
    blocks_ref,
    table_ref,
    out_ref,
    anchor_ref,
    cells,
    patch,
    layers,
    nodes,
    near,
    total,
    sem,
):
    copy = pltpu.make_async_copy(ints_ref.at[16:24], anchor_ref, sem)
    copy.start()
    near[...] = jnp.zeros_like(near)
    picks = layer_picks(ints_ref[16:19, 0:TILES])
    tab = halves(table_ref[...])
    phase_high = mm(tab[0], picks).T.astype(BF16)
    phase_low = mm(tab[1], picks).T.astype(BF16)
    data = in_ref[...]
    field = mm(phase_high, data) + mm(phase_low, data)
    cells[...] = field.astype(BF16).astype(F32)
    copy.wait()
    sign = jnp.where(iota((2, 128), 0) == 0, -1.0, 1.0)
    for q in range(8):
        source = slots_ref[pl.ds(anchor_ref[5, q] * 2, 2), :]
        turn = jnp.concatenate([source[1:2], source[0:1]], axis=0) * sign
        value = mm_nt(source.astype(BF16), blocks_ref[q, 0]) + mm_nt(turn.astype(BF16), blocks_ref[q, 1])
        target = pl.ds(anchor_ref[4, q] * 2, 2)
        near[target, :] = near[target, :] + value
    for t in range(TILES):
        odd, starts = place(anchor_ref, t)
        parts = []
        for h in range(2):
            lane = pl.multiple_of((starts[h] >> 7) * 128, 128)
            wide = cells[128 * h + 8 * t : 128 * h + 8 * t + 8, pl.ds(lane, 256)]
            parts.append(pltpu.roll(wide, (256 - (starts[h] & 127)) & 255, 1)[:, 0:128])
        patch[8 * t : 8 * t + 8, 0:128] = jnp.where(odd == 1, parts[1], parts[0])
        patch[8 * t : 8 * t + 8, 128:256] = jnp.where(odd == 1, parts[0], parts[1])
    value = mm_nt(patch[...].astype(BF16), node_lanes())
    layers[0:128, :] = value[:, 0:128]
    layers[128:256, :] = value[:, 128:256]
    layer = iota((32, 128), 1) % 4
    for half in range(2):
        value = layers[pl.ds(128 * half, 32, stride=4), :]
        for b in range(1, 4):
            value = jnp.where(layer == b, layers[pl.ds(128 * half + b, 32, stride=4), :], value)
        nodes[:, 128 * half : 128 * half + 128] = value
    for t in range(TILES):
        total[2 * t : 2 * t + 2, :] = mm(nodes[2 * t : 2 * t + 2, :].astype(BF16), proj_ref[t])
    high, low = halves(total[...] + near[...])
    slot = as_row(ints_ref[0 : SOURCES // 128, :])
    pick = slot_picks(slot)
    value = mm(high, pick) + mm(low, pick)
    value = jnp.where(iota((32, SOURCES), 0) // 2 == (slot >> 7), value, 0.0)
    value = value[0:8] + value[8:16] + value[16:24] + value[24:32]
    value = value + pltpu.roll(value, 4, 0)
    value = value + pltpu.roll(value, 2, 0)
    out_ref[...] = value[0:2]


VM = pl.BlockSpec(memory_space=pltpu.VMEM)
HB = pl.BlockSpec(memory_space=pltpu.HBM)


def call(kernel, outs, in_specs, scratch, flops, moved, limit=VMEM_LIMIT):
    return pl.pallas_call(
        kernel,
        out_shape=[shape(*out.shape, dtype=out.dtype) for out in outs],
        in_specs=in_specs,
        out_specs=[VM] * len(outs),
        scratch_shapes=scratch,
        compiler_params=pltpu.CompilerParams(vmem_limit_bytes=limit),
        cost_estimate=pl.CostEstimate(flops=flops, bytes_accessed=moved, transcendentals=0),
    )


def shape(*dims, dtype=F32):
    return jax.ShapeDtypeStruct(dims, dtype)


def swap(cells, axis, rows):
    parts = lax.axis_size(axis)
    moved = lax.all_to_all(cells.reshape(parts, rows, -1), axis, 0, 0, tiled=True)
    return moved.reshape(parts * rows, -1)


def body(charges, source_slot, tile_anchor, projection, near_pairs, near_blocks, green_real, green_imag):
    first, z_back = z_tables()
    y_table, y_back = y_tables()
    block = pltpu.VMEM((512, 128), F32)
    cells, slots, ints = call(
        spread_kernel,
        [shape(128, CELLS, dtype=BF16), shape(32, SLOTS), shape(24, 128, dtype=jnp.int32)],
        [HB] * 6,
        [
            pltpu.VMEM((2, SOURCES), F32),
            pltpu.VMEM((SOURCES // 128, 128), jnp.int32),
            pltpu.SMEM((3, TILES), jnp.int32),
            pltpu.VMEM((3, TILES), jnp.int32),
            pltpu.VMEM((2, PAIRS), jnp.int32),
            pltpu.VMEM((TILES, 256, SLOTS), BF16),
            pltpu.VMEM((384, 256), BF16),
            pltpu.VMEM((32, 256), F32),
            pltpu.VMEM((256, 128), F32),
            pltpu.VMEM((128, 256), F32),
            pltpu.VMEM((256, CELLS), F32),
            pltpu.SemaphoreType.DMA((7,)),
        ],
        10**9,
        2 * 10**6,
        LIMIT_A,
    )(charges, source_slot.reshape(SOURCES // 128, 128), tile_anchor.T, near_pairs.T, projection, first)
    cells = swap(cells, "gy", 8)
    lines = shape(512, 128, dtype=BF16)
    lines = call(y_kernel, [lines], [VM] * 2, [block], 10**8, 10**6)(cells, y_table)[0]
    lines = swap(lines, "gx", UPAD)
    lines = call(x_kernel, [lines], [VM] * 4, [block] * 2, 10**8, 10**6)(
        lines, green_real.transpose(1, 2, 0), green_imag.transpose(1, 2, 0), x_tables()
    )[0]
    lines = swap(lines, "gx", UPAD)
    cells = call(y_back_kernel, [cells], [VM] * 2, [block] * 2, 10**8, 10**6)(lines, y_back)[0]
    cells = swap(cells, "gy", 8)
    return call(
        gather_kernel,
        [shape(2, SOURCES)],
        [VM] * 6,
        [
            pltpu.SMEM((8, 128), jnp.int32),
            pltpu.VMEM((256, CELLS), F32),
            pltpu.VMEM((128, 256), F32),
            pltpu.VMEM((256, 128), F32),
            pltpu.VMEM((32, 256), F32),
            pltpu.VMEM((32, SLOTS), F32),
            pltpu.VMEM((32, SLOTS), F32),
            pltpu.SemaphoreType.DMA,
        ],
        10**9,
        2 * 10**6,
    )(cells, ints, projection, slots, near_blocks, z_back)[0]


def solution(mesh):
    return jax.shard_map(
        body,
        mesh=mesh,
        in_specs=(
            P(None, ("gx", "gy")),
            P(("gx", "gy")),
            P(("gx", "gy"), None),
            P(("gx", "gy"), None, None),
            P(("gx", "gy"), None),
            P(("gx", "gy"), None, None, None),
            P(None, "gx", "gy"),
            P(None, "gx", "gy"),
        ),
        out_specs=P(None, ("gx", "gy")),
        check_vma=False,
    )
```

```python
import math

import jax
import jax.numpy as jnp
import ml_dtypes
import numpy as np
from jax import lax
from jax.experimental import pallas as pl
from jax.experimental.pallas import tpu as pltpu
from jax.sharding import PartitionSpec as P

TILES = 16
SLOTS = 128
PAIRS = 8
SOURCES = 1536
NU = 12
LINES = (96, 4, 128)
ORDER_X = (1, 10, 13, 25, 21, 8, 15, 26, 7, 0, 28, 18, 6, 4, 20, 24, 12, 16, 3, 2, 31, 14, 23, 29, 5, 11, 17, 27, 30, 22, 9, 19)
ORDER_Y = tuple(2 * z + x for x in range(2) for z in range(8))
NV = 40
CELLS = 512
F32 = jnp.float32
BF16 = jnp.bfloat16
VMEM_LIMIT = 16 * 1024 * 1024
LIMIT_A = 65536 * 1024 - 960 * 1024


def split_table(table):
    high = table.astype(np.float32).astype(ml_dtypes.bfloat16)
    low = (table - high.astype(np.float64)).astype(np.float32).astype(ml_dtypes.bfloat16)
    return high, low


def as_real(theta, inverse):
    sign = -1.0 if inverse else 1.0
    cos, sin = np.cos(theta), sign * np.sin(theta)
    return np.stack([np.stack([cos, sin], -1), np.stack([-sin, cos], -1)], -2)


def z_tables():
    kz = np.arange(32)
    theta = 2.0 * np.pi * (np.outer(kz, kz) % 32) / 32
    forward = as_real(theta, False).reshape(16, 2, 32, 2, 2)[list(ORDER_Y)]
    table = np.einsum("jqzoc,hg->jhqogcz", forward, np.eye(2)).reshape(128, 128)
    backward = as_real(theta, True).reshape(16, 2, 32, 2, 2)[list(ORDER_Y)] / 32.0
    table_back = np.einsum("jqzoc,hg->jhqcgoz", backward, np.eye(2)).reshape(128, 128)
    first = np.zeros((4096, 256), ml_dtypes.bfloat16)
    p = np.arange(256)
    first[p, (p // 32 % 2) * 128 + (p // 64) * NV + p // 4 % 8] = 1.0
    first[256:384, 0:128], first[256:384, 128:256] = split_table(table)
    return jnp.asarray(first), in_rows(table_back)


def in_rows(*tables):
    padded = [np.pad(table, ((0, 0), (0, 128 - table.shape[1]))) for table in tables]
    return jnp.asarray(np.concatenate(padded, 0).astype(np.float32))


def y_tables():
    k = np.arange(16)
    theta = 2.0 * np.pi * (np.outer(k, np.array(ORDER_Y)) % 16) / 16
    eyes = np.einsum("hg,qr->hgqr", np.eye(2), np.eye(2))
    table = np.einsum("kjoc,hgqr->jhqcgokr", as_real(theta, False), eyes).reshape(128, 128)
    table_back = np.einsum("kjoc,hgqr->jgrohckq", as_real(theta, True) / 512.0, eyes).reshape(128, 128)
    phi = 2.0 * np.pi * np.outer(np.arange(NV) - 4, k) / 512
    wide = np.broadcast_to(phi[:, None, None, :, None], (NV, 2, 2, 16, 2)).reshape(NV, 128)
    psi = 2.0 * np.pi * (np.outer(np.array(ORDER_X), np.arange(NV) - 4) % 32) / 32
    rows = np.concatenate([np.cos(psi), np.sin(psi)], 1)
    rows_back = np.concatenate([np.cos(psi.T), -np.sin(psi.T)], 1)
    turn = (np.cos(wide), np.sin(wide))
    return in_rows(*turn, table, rows), in_rows(*turn, table_back, rows_back)


def x_tables():
    k0 = np.arange(32)
    alpha = 2.0 * np.pi * (np.outer(k0, np.array(ORDER_X)) % 32) / 32
    rows = np.concatenate([np.cos(alpha), np.sin(alpha)], 1)
    rows_back = np.concatenate([np.cos(alpha.T), -np.sin(alpha.T)], 1) / 512.0
    beta = 2.0 * np.pi * np.outer(k0, np.arange(NU) - 2) / 256
    phi = 2.0 * np.pi * (k0[:, None] + 32 * np.arange(8)[None, :]) / 512
    return in_rows(rows, rows_back, np.concatenate([np.cos(beta), np.sin(beta), np.cos(phi), np.sin(phi)], 1))


def mm(a, b):
    return lax.dot_general(a, b, (((1,), (0,)), ((), ())), preferred_element_type=F32)


def mm_nt(a, b):
    return lax.dot_general(a, b, (((1,), (1,)), ((), ())), preferred_element_type=F32)


def halves(value):
    high = value.astype(BF16)
    return high, (value - high.astype(F32)).astype(BF16)


def iota(shape, axis):
    return lax.broadcasted_iota(jnp.int32, shape, axis)


def turned(value):
    bit = (iota(value.shape, 1) // 32) % 2
    return jnp.where(bit == 0, pltpu.roll(value, 96, 1), -pltpu.roll(value, 32, 1))


def crossed(value):
    half = iota(value.shape, 1) // 64
    return pltpu.roll(value, 64, 1) + jnp.where(half == 0, value, -value)


def layer_picks(anchor):
    fan = jnp.where(iota((TILES, 256), 0) == (iota((TILES, 256), 1) // 8) % TILES, 1.0, 0.0).astype(BF16)
    low = mm(anchor[2:3, :].astype(F32).astype(BF16), fan)
    at = iota((1, 256), 1)
    want = low + ((at // 128) * 64 + ((at // 4) % 2) * 32 + at % 4).astype(F32)
    return jnp.where(iota((128, 256), 0) == want.astype(jnp.int32), 1.0, 0.0).astype(BF16)


def place(anchor_ref, t):
    x = (anchor_ref[0, t] & 15) + 1
    y = (anchor_ref[1, t] & 31) + 1
    starts = (((x + 1) >> 1) * NV + y, (x >> 1) * NV + y)
    return x & 1, starts


def as_row(slot):
    return jnp.concatenate([slot[r : r + 1, :] for r in range(SOURCES // 128)], axis=1)


def slot_picks(slot):
    return jnp.where(iota((SLOTS, SOURCES), 0) == (slot & 127), 1.0, 0.0).astype(BF16)


def spread_kernel(
    charges_hbm,
    slot_hbm,
    anchor_hbm,
    pairs_hbm,
    proj_hbm,
    tables_hbm,
    out_ref,
    slots_ref,
    ints_ref,
    charges_ref,
    slot_ref,
    anchor_ref,
    anchor_vec,
    pairs_vec,
    proj_ref,
    tables_ref,
    nodes,
    layers,
    patch,
    cells,
    sems,
):
    fetched = (
        (charges_hbm, charges_ref),
        (slot_hbm, slot_ref),
        (anchor_hbm, anchor_ref),
        (anchor_hbm, anchor_vec),
        (pairs_hbm, pairs_vec),
        (proj_hbm, proj_ref),
        (tables_hbm.at[0:384], tables_ref),
    )
    copies = [pltpu.make_async_copy(src, dst, sems.at[n]) for n, (src, dst) in enumerate(fetched)]
    for copy in copies:
        copy.start()
    cells[...] = jnp.zeros_like(cells)
    for copy in copies[:5]:
        copy.wait()
    ints_ref[...] = jnp.zeros_like(ints_ref)
    ints_ref[0 : SOURCES // 128, :] = slot_ref[...]
    ints_ref[16:19, 0:TILES] = anchor_vec[...]
    ints_ref[20:22, 0:PAIRS] = pairs_vec[...]
    slot = as_row(slot_ref[...])
    row = iota((32, SOURCES), 0)
    charge = jnp.where(row % 2 == 0, charges_ref[0:1, :], charges_ref[1:2, :])
    held = jnp.where(row // 2 == (slot >> 7), charge, 0.0).astype(BF16)
    slots_ref[...] = mm_nt(held, slot_picks(slot))
    picks = layer_picks(anchor_vec[...])
    copies[5].wait()
    for t in range(TILES):
        nodes[2 * t : 2 * t + 2, :] = mm_nt(slots_ref[2 * t : 2 * t + 2, :].astype(BF16), proj_ref[t])
    value = nodes[...]
    layer = iota((32, 128), 1) % 4
    for half in range(2):
        for b in range(4):
            part = value[:, 128 * half : 128 * half + 128]
            layers[pl.ds(128 * half + b, 32, stride=4), :] = jnp.where(layer == b, part, 0.0)
    high, low = halves(jnp.concatenate([layers[0:128, :], layers[128:256, :]], axis=1))
    copies[6].wait()
    spread = tables_ref[0:256, :]
    patch[...] = mm(high, spread) + mm(low, spread)
    empty = jnp.zeros((8, 128), F32)
    for t in range(TILES):
        odd, starts = place(anchor_ref, t)
        even_part = patch[8 * t : 8 * t + 8, 0:128]
        odd_part = patch[8 * t : 8 * t + 8, 128:256]
        parts = (jnp.where(odd == 1, odd_part, even_part), jnp.where(odd == 1, even_part, odd_part))
        for h in range(2):
            wide = jnp.concatenate([parts[h], empty], axis=1)
            wide = pltpu.roll(wide, starts[h] & 127, 1)
            lane = pl.multiple_of((starts[h] >> 7) * 128, 128)
            cells[128 * h + 8 * t : 128 * h + 8 * t + 8, pl.ds(lane, 256)] = wide
    phase_high = mm(tables_ref[256:384, 0:128], picks).astype(BF16)
    phase_low = mm(tables_ref[256:384, 128:256], picks).astype(BF16)
    high, low = halves(cells[...])
    out = mm(phase_high, high) + mm(phase_high, low) + mm(phase_low, high)
    out_ref[...] = out.astype(BF16)


def y_kernel(in_ref, table_ref, out_ref, hold):
    data = in_ref[...].astype(F32).T.astype(BF16)
    cos, sin = table_ref[0:NV, :], table_ref[NV : 2 * NV, :]
    table = table_ref[2 * NV : 2 * NV + 128, :]
    high, low = halves(jnp.concatenate([table, turned(table)], axis=1))
    both = mm(data, high) + mm(data, low)
    rows = halves(table_ref[2 * NV + 128 : 2 * NV + 160, 0 : 2 * NV])
    for u in range(NU):
        plain = both[NV * u : NV * (u + 1), 0:128]
        turn = both[NV * u : NV * (u + 1), 128:256]
        lines = jnp.concatenate([plain * cos + turn * sin, turn * cos - plain * sin], axis=0)
        high, low = halves(lines)
        out = mm(rows[0], high) + mm(rows[0], low) + mm(rows[1], high)
        hold[pl.ds(u, 32, stride=NU), :] = out
    out_ref[...] = hold[...].reshape(LINES).astype(BF16)


def rotated(value, cos, sin):
    plain, turn = value
    return plain * cos + turn * sin, turn * cos - plain * sin


def eighths(value, count, sign):
    plain, turn = value
    if count == 0:
        return value
    if count == 2:
        return (turn, -plain) if sign > 0 else (-turn, plain)
    if count == 3:
        return eighths(eighths(value, 2, sign), 1, sign)
    root = math.sqrt(0.5)
    if sign > 0:
        return (plain + turn) * root, (turn - plain) * root
    return (plain - turn) * root, (turn + plain) * root


def short_dft(values, sign):
    count = len(values)
    if count == 1:
        return values
    even, odd = short_dft(values[0::2], sign), short_dft(values[1::2], sign)
    odd = [eighths(value, 8 // count * n, sign) for n, value in enumerate(odd)]
    sums = [(a[0] + b[0], a[1] + b[1]) for a, b in zip(even, odd)]
    return sums + [(a[0] - b[0], a[1] - b[1]) for a, b in zip(even, odd)]


def line_pair(rows, plain, turn):
    four = jnp.concatenate(
        [jnp.concatenate([plain, turn], axis=1), jnp.concatenate([turn, -plain], axis=1)], axis=0
    ).astype(BF16)
    return mm(rows[0], four) + mm(rows[1], four)


def x_kernel(in_ref, real_ref, imag_ref, table_ref, out_ref, hold, hold_turned):
    into = halves(table_ref[0:32, 0:64])
    back = halves(table_ref[32:64, 0:64])
    angles = table_ref[64:96, :]
    second = iota((32, 128), 1) >= 64

    def step(u):
        shape = (32, 128)
        cos, sin = angles[:, u : u + 1], angles[:, NU + u : NU + u + 1]
        return jnp.broadcast_to(cos, shape), jnp.broadcast_to(sin, shape)

    def fold(n):
        n = n + 2 * NU
        return jnp.where(second, angles[:, n : n + 1], 1.0), jnp.where(second, angles[:, n + 8 : n + 9], 0.0)

    data = in_ref[...].astype(F32).reshape(384, 128)
    hold[...] = data
    hold_turned[...] = turned(data)
    classes = [None] * 8
    for u in range(NU):
        plain = hold[pl.ds(u, 32, stride=NU), :]
        both = line_pair(into, plain, hold_turned[pl.ds(u, 32, stride=NU), :])
        value = rotated((both[:, 0:128], both[:, 128:256]), *step(u))
        at = (u - 2) % 8
        classes[at] = value if classes[at] is None else tuple(a + b for a, b in zip(classes[at], value))
    lines = short_dft(classes, 1)

    def wide(green):
        green = green.reshape(32, 512)
        first, second = green[:, 0:256], green[:, 256:512]
        return jnp.concatenate([first, first, second, second], axis=0).T

    real, imag = wide(real_ref[...]), wide(imag_ref[...])
    for n in range(8):
        rows = slice(32 * n, 32 * n + 32)
        cos, sin = fold(n)
        plain, turn = rotated(lines[n], cos, sin)
        plain, turn = crossed(plain), crossed(turn)
        plain, turn = plain * real[rows] - turn * imag[rows], turn * real[rows] + plain * imag[rows]
        lines[n] = rotated((crossed(plain), crossed(turn)), cos, -sin)
    classes = short_dft(lines, -1)
    for u in range(NU):
        cos, sin = step(u)
        value = rotated(classes[(u - 2) % 8], cos, -sin)
        high, low = halves(jnp.concatenate(value, axis=0))
        out = mm(back[0], high) + mm(back[0], low) + mm(back[1], high)
        hold[pl.ds(u, 32, stride=NU), :] = out
    out_ref[...] = hold[...].reshape(LINES).astype(BF16)


def y_back_kernel(in_ref, table_ref, out_ref, hold, hold_turned):
    data = in_ref[...].astype(F32).reshape(384, 128)
    hold[...] = data
    hold_turned[...] = turned(data)
    cos, sin = table_ref[0:NV, :], table_ref[NV : 2 * NV, :]
    tab = halves(table_ref[2 * NV : 2 * NV + 128, :])
    rows = halves(table_ref[2 * NV + 128 : 3 * NV + 128, 0:64])
    lines = []
    for u in range(NU):
        plain = hold[pl.ds(u, 32, stride=NU), :]
        turn = hold_turned[pl.ds(u, 32, stride=NU), :]
        both = line_pair(rows, plain, turn)
        lines.append(both[:, 0:128] * cos - both[:, 128:256] * sin)
    lines.append(jnp.zeros((CELLS - NU * NV, 128), F32))
    high, low = halves(jnp.concatenate(lines, axis=0))
    out = mm_nt(tab[0], high) + mm_nt(tab[0], low) + mm_nt(tab[1], high)
    out_ref[...] = out.astype(BF16)


def node_lanes():
    node = iota((256, 256), 0)
    lane = ((node >> 5) & 1) * 128 + (node >> 6) * NV + ((node >> 2) & 7)
    return jnp.where(iota((256, 256), 1) == lane, 1.0, 0.0).astype(BF16)


def gather_kernel(
    in_ref,
    ints_ref,
    proj_ref,
    slots_ref,
    blocks_ref,
    table_ref,
    out_ref,
    anchor_ref,
    cells,
    patch,
    layers,
    nodes,
    near,
    total,
    sem,
):
    copy = pltpu.make_async_copy(ints_ref.at[16:24], anchor_ref, sem)
    copy.start()
    near[...] = jnp.zeros_like(near)
    picks = layer_picks(ints_ref[16:19, 0:TILES])
    tab = halves(table_ref[...])
    phase_high = mm(tab[0], picks).T.astype(BF16)
    phase_low = mm(tab[1], picks).T.astype(BF16)
    data = in_ref[...]
    field = mm(phase_high, data) + mm(phase_low, data)
    cells[...] = field.astype(BF16).astype(F32)
    copy.wait()
    sign = jnp.where(iota((2, 128), 0) == 0, -1.0, 1.0)
    for q in range(8):
        source = slots_ref[pl.ds(anchor_ref[5, q] * 2, 2), :]
        turn = jnp.concatenate([source[1:2], source[0:1]], axis=0) * sign
        value = mm_nt(source.astype(BF16), blocks_ref[q, 0]) + mm_nt(turn.astype(BF16), blocks_ref[q, 1])
        target = pl.ds(anchor_ref[4, q] * 2, 2)
        near[target, :] = near[target, :] + value
    for t in range(TILES):
        odd, starts = place(anchor_ref, t)
        parts = []
        for h in range(2):
            lane = pl.multiple_of((starts[h] >> 7) * 128, 128)
            wide = cells[128 * h + 8 * t : 128 * h + 8 * t + 8, pl.ds(lane, 256)]
            parts.append(pltpu.roll(wide, (256 - (starts[h] & 127)) & 255, 1)[:, 0:128])
        patch[8 * t : 8 * t + 8, 0:128] = jnp.where(odd == 1, parts[1], parts[0])
        patch[8 * t : 8 * t + 8, 128:256] = jnp.where(odd == 1, parts[0], parts[1])
    value = mm_nt(patch[...].astype(BF16), node_lanes())
    layers[0:128, :] = value[:, 0:128]
    layers[128:256, :] = value[:, 128:256]
    layer = iota((32, 128), 1) % 4
    for half in range(2):
        value = layers[pl.ds(128 * half, 32, stride=4), :]
        for b in range(1, 4):
            value = jnp.where(layer == b, layers[pl.ds(128 * half + b, 32, stride=4), :], value)
        nodes[:, 128 * half : 128 * half + 128] = value
    for t in range(TILES):
        total[2 * t : 2 * t + 2, :] = mm(nodes[2 * t : 2 * t + 2, :].astype(BF16), proj_ref[t])
    high, low = halves(total[...] + near[...])
    slot = as_row(ints_ref[0 : SOURCES // 128, :])
    pick = slot_picks(slot)
    value = mm(high, pick) + mm(low, pick)
    value = jnp.where(iota((32, SOURCES), 0) // 2 == (slot >> 7), value, 0.0)
    value = value[0:8] + value[8:16] + value[16:24] + value[24:32]
    value = value + pltpu.roll(value, 4, 0)
    value = value + pltpu.roll(value, 2, 0)
    out_ref[...] = value[0:2]


VM = pl.BlockSpec(memory_space=pltpu.VMEM)
HB = pl.BlockSpec(memory_space=pltpu.HBM)


def call(kernel, outs, in_specs, scratch, flops, moved, limit=VMEM_LIMIT):
    return pl.pallas_call(
        kernel,
        out_shape=[shape(*out.shape, dtype=out.dtype) for out in outs],
        in_specs=in_specs,
        out_specs=[VM] * len(outs),
        scratch_shapes=scratch,
        compiler_params=pltpu.CompilerParams(vmem_limit_bytes=limit),
        cost_estimate=pl.CostEstimate(flops=flops, bytes_accessed=moved, transcendentals=0),
    )


def shape(*dims, dtype=F32):
    return jax.ShapeDtypeStruct(dims, dtype)


def swap(cells, axis):
    parts = lax.axis_size(axis)
    blocks = cells.reshape((parts, -1) + cells.shape[1:] if cells.ndim == 3 else (parts, 8, -1))
    order = ORDER_X if axis == "gx" else ORDER_Y
    moved = lax.all_to_all(blocks, axis, 0, 0, axis_index_groups=[list(order)], tiled=True)
    return moved.reshape(cells.shape)


def body(charges, source_slot, tile_anchor, projection, near_pairs, near_blocks, green_real, green_imag):
    first, z_back = z_tables()
    y_table, y_back = y_tables()
    block = pltpu.VMEM((384, 128), F32)
    cells, slots, ints = call(
        spread_kernel,
        [shape(128, CELLS, dtype=BF16), shape(32, SLOTS), shape(24, 128, dtype=jnp.int32)],
        [HB] * 6,
        [
            pltpu.VMEM((2, SOURCES), F32),
            pltpu.VMEM((SOURCES // 128, 128), jnp.int32),
            pltpu.SMEM((3, TILES), jnp.int32),
            pltpu.VMEM((3, TILES), jnp.int32),
            pltpu.VMEM((2, PAIRS), jnp.int32),
            pltpu.VMEM((TILES, 256, SLOTS), BF16),
            pltpu.VMEM((384, 256), BF16),
            pltpu.VMEM((32, 256), F32),
            pltpu.VMEM((256, 128), F32),
            pltpu.VMEM((128, 256), F32),
            pltpu.VMEM((256, CELLS), F32),
            pltpu.SemaphoreType.DMA((7,)),
        ],
        10**9,
        2 * 10**6,
        LIMIT_A,
    )(charges, source_slot.reshape(SOURCES // 128, 128), tile_anchor.T, near_pairs.T, projection, first)
    cells = swap(cells, "gy")
    lines = shape(*LINES, dtype=BF16)
    lines = call(y_kernel, [lines], [VM] * 2, [block], 10**9, 10**6)(cells, y_table)[0]
    lines = swap(lines, "gx")
    lines = call(x_kernel, [lines], [VM] * 4, [block] * 2, 10**9, 10**6)(
        lines, green_real.transpose(1, 2, 0), green_imag.transpose(1, 2, 0), x_tables()
    )[0]
    lines = swap(lines, "gx")
    cells = call(y_back_kernel, [cells], [VM] * 2, [block] * 2, 10**9, 10**6)(lines, y_back)[0]
    cells = swap(cells, "gy")
    return call(
        gather_kernel,
        [shape(2, SOURCES)],
        [VM] * 6,
        [
            pltpu.SMEM((8, 128), jnp.int32),
            pltpu.VMEM((256, CELLS), F32),
            pltpu.VMEM((128, 256), F32),
            pltpu.VMEM((256, 128), F32),
            pltpu.VMEM((32, 256), F32),
            pltpu.VMEM((32, SLOTS), F32),
            pltpu.VMEM((32, SLOTS), F32),
            pltpu.SemaphoreType.DMA,
        ],
        10**9,
        2 * 10**6,
    )(cells, ints, projection, slots, near_blocks, z_back)[0]


def solution(mesh):
    return jax.shard_map(
        body,
        mesh=mesh,
        in_specs=(
            P(None, ("gx", "gy")),
            P(("gx", "gy")),
            P(("gx", "gy"), None),
            P(("gx", "gy"), None, None),
            P(("gx", "gy"), None),
            P(("gx", "gy"), None, None, None),
            P(None, "gx", "gy"),
            P(None, "gx", "gy"),
        ),
        out_specs=P(None, ("gx", "gy")),
        check_vma=False,
    )
```

```python
import math

import jax
import jax.numpy as jnp
import ml_dtypes
import numpy as np
from jax import lax
from jax.experimental import pallas as pl
from jax.experimental.pallas import tpu as pltpu
from jax.sharding import PartitionSpec as P

TILES = 16
SLOTS = 128
PAIRS = 8
SOURCES = 1536
NU = 12
LINES = (96, 4, 128)
ORDER_X = (1, 10, 13, 25, 21, 8, 15, 26, 7, 0, 28, 18, 6, 4, 20, 24, 12, 16, 3, 2, 31, 14, 23, 29, 5, 11, 17, 27, 30, 22, 9, 19)
ORDER_Y = tuple(2 * z + x for x in range(2) for z in range(8))
NV = 40
CELLS = 512
F32 = jnp.float32
BF16 = jnp.bfloat16
VMEM_LIMIT = 16 * 1024 * 1024


def split_table(table):
    high = table.astype(np.float32).astype(ml_dtypes.bfloat16)
    low = (table - high.astype(np.float64)).astype(np.float32).astype(ml_dtypes.bfloat16)
    return high, low


def as_real(theta, inverse):
    sign = -1.0 if inverse else 1.0
    cos, sin = np.cos(theta), sign * np.sin(theta)
    return np.stack([np.stack([cos, sin], -1), np.stack([-sin, cos], -1)], -2)


def z_tables():
    kz = np.arange(32)
    theta = 2.0 * np.pi * (np.outer(kz, kz) % 32) / 32
    forward = as_real(theta, False).reshape(16, 2, 32, 2, 2)[list(ORDER_Y)]
    table = np.einsum("jqzoc,hg->jhqogcz", forward, np.eye(2)).reshape(128, 128)
    backward = as_real(theta, True).reshape(16, 2, 32, 2, 2)[list(ORDER_Y)] / 32.0
    table_back = np.einsum("jqzoc,hg->jhqcgoz", backward, np.eye(2)).reshape(128, 128)
    first = np.zeros((384, 256), ml_dtypes.bfloat16)
    p = np.arange(256)
    first[p, (p // 32 % 2) * 128 + (p // 64) * NV + p // 4 % 8] = 1.0
    first[256:384, 0:128], first[256:384, 128:256] = split_table(table)
    return jnp.asarray(first), in_rows(table_back)


def in_rows(*tables):
    padded = [np.pad(table, ((0, 0), (0, 128 - table.shape[1]))) for table in tables]
    return jnp.asarray(np.concatenate(padded, 0).astype(np.float32))


def y_tables():
    k = np.arange(16)
    theta = 2.0 * np.pi * (np.outer(k, np.array(ORDER_Y)) % 16) / 16
    eyes = np.einsum("hg,qr->hgqr", np.eye(2), np.eye(2))
    table = np.einsum("kjoc,hgqr->jhqcgokr", as_real(theta, False), eyes).reshape(128, 128)
    table_back = np.einsum("kjoc,hgqr->jgrohckq", as_real(theta, True) / 512.0, eyes).reshape(128, 128)
    phi = 2.0 * np.pi * np.outer(np.arange(NV) - 4, k) / 512
    wide = np.broadcast_to(phi[:, None, None, :, None], (NV, 2, 2, 16, 2)).reshape(NV, 128)
    psi = 2.0 * np.pi * (np.outer(np.array(ORDER_X), np.arange(NV) - 4) % 32) / 32
    rows = np.concatenate([np.cos(psi), np.sin(psi)], 1)
    rows_back = np.concatenate([np.cos(psi.T), -np.sin(psi.T)], 1)
    turn = (np.cos(wide), np.sin(wide))
    return in_rows(*turn, table, rows), in_rows(*turn, table_back, rows_back)


def x_tables():
    k0 = np.arange(32)
    alpha = 2.0 * np.pi * (np.outer(k0, np.array(ORDER_X)) % 32) / 32
    rows = np.concatenate([np.cos(alpha), np.sin(alpha)], 1)
    rows_back = np.concatenate([np.cos(alpha.T), -np.sin(alpha.T)], 1) / 512.0
    beta = 2.0 * np.pi * np.outer(k0, np.arange(NU) - 2) / 256
    phi = 2.0 * np.pi * (k0[:, None] + 32 * np.arange(8)[None, :]) / 512
    return in_rows(rows, rows_back, np.concatenate([np.cos(beta), np.sin(beta), np.cos(phi), np.sin(phi)], 1))


def mm(a, b):
    return lax.dot_general(a, b, (((1,), (0,)), ((), ())), preferred_element_type=F32)


def mm_nt(a, b):
    return lax.dot_general(a, b, (((1,), (1,)), ((), ())), preferred_element_type=F32)


def halves(value):
    high = value.astype(BF16)
    return high, (value - high.astype(F32)).astype(BF16)


def iota(shape, axis):
    return lax.broadcasted_iota(jnp.int32, shape, axis)


def turned(value):
    bit = (iota(value.shape, 1) // 32) % 2
    return jnp.where(bit == 0, pltpu.roll(value, 96, 1), -pltpu.roll(value, 32, 1))


def crossed(value):
    half = iota(value.shape, 1) // 64
    return pltpu.roll(value, 64, 1) + jnp.where(half == 0, value, -value)


def layer_picks(anchor):
    fan = jnp.where(iota((TILES, 256), 0) == (iota((TILES, 256), 1) // 8) % TILES, 1.0, 0.0).astype(BF16)
    low = mm(anchor[2:3, :].astype(F32).astype(BF16), fan)
    at = iota((1, 256), 1)
    want = low + ((at // 128) * 64 + ((at // 4) % 2) * 32 + at % 4).astype(F32)
    return jnp.where(iota((128, 256), 0) == want.astype(jnp.int32), 1.0, 0.0).astype(BF16)


def place(anchor_ref, t):
    x = (anchor_ref[0, t] & 15) + 1
    y = (anchor_ref[1, t] & 31) + 1
    starts = (((x + 1) >> 1) * NV + y, (x >> 1) * NV + y)
    return x & 1, starts


def as_row(slot):
    return jnp.concatenate([slot[r : r + 1, :] for r in range(SOURCES // 128)], axis=1)


def slot_picks(slot):
    return jnp.where(iota((SLOTS, SOURCES), 0) == (slot & 127), 1.0, 0.0).astype(BF16)


def side_by_side(ref, n):
    return jnp.concatenate([ref[n], ref[n + 1]], axis=1)


def spread_kernel(
    charges_hbm,
    slot_hbm,
    anchor_hbm,
    pairs_hbm,
    proj_hbm,
    tables_hbm,
    out_ref,
    slots_ref,
    ints_ref,
    charges_ref,
    slot_ref,
    anchor_ref,
    anchor_vec,
    pairs_vec,
    proj_ref,
    tables_ref,
    nodes,
    layers,
    patch,
    cells,
    sems,
):
    fetched = (
        (charges_hbm, charges_ref),
        (slot_hbm, slot_ref),
        (anchor_hbm, anchor_ref),
        (anchor_hbm, anchor_vec),
        (pairs_hbm, pairs_vec),
    ) + tuple((proj_hbm.at[n : n + 4], proj_ref.at[n : n + 4]) for n in range(0, TILES, 4))
    fetched = fetched + ((tables_hbm, tables_ref),)
    copies = [pltpu.make_async_copy(src, dst, sems.at[n]) for n, (src, dst) in enumerate(fetched)]
    for copy in copies:
        copy.start()
    cells[...] = jnp.zeros_like(cells)
    for copy in copies[:5]:
        copy.wait()
    ints_ref[...] = jnp.zeros_like(ints_ref)
    ints_ref[0 : SOURCES // 128, :] = slot_ref[...]
    ints_ref[16:19, 0:TILES] = anchor_vec[...]
    ints_ref[20:22, 0:PAIRS] = pairs_vec[...]
    slot = as_row(slot_ref[...])
    row = iota((32, SOURCES), 0)
    charge = jnp.where(row % 2 == 0, charges_ref[0:1, :], charges_ref[1:2, :])
    held = jnp.where(row // 2 == (slot >> 7), charge, 0.0).astype(BF16)
    slots_ref[...] = mm_nt(held, slot_picks(slot))
    picks = layer_picks(anchor_vec[...])
    first = iota((4, SLOTS), 0) < 2
    for t in range(0, TILES, 2):
        if t % 4 == 0:
            copies[5 + t // 4].wait()
        mine = slots_ref[2 * t : 2 * t + 4, :]
        mine = jnp.concatenate([jnp.where(first, mine, 0.0), jnp.where(first, 0.0, mine)], axis=1)
        nodes[2 * t : 2 * t + 4, :] = mm_nt(mine.astype(BF16), side_by_side(proj_ref, t))
    value = nodes[...]
    layer = iota((32, 128), 1) % 4
    for half in range(2):
        for b in range(4):
            part = value[:, 128 * half : 128 * half + 128]
            layers[pl.ds(128 * half + b, 32, stride=4), :] = jnp.where(layer == b, part, 0.0)
    high, low = halves(jnp.concatenate([layers[0:128, :], layers[128:256, :]], axis=1))
    copies[9].wait()
    spread = tables_ref[0:256, :]
    patch[...] = mm(high, spread) + mm(low, spread)
    empty = jnp.zeros((8, 128), F32)
    for t in range(TILES):
        odd, starts = place(anchor_ref, t)
        even_part = patch[8 * t : 8 * t + 8, 0:128]
        odd_part = patch[8 * t : 8 * t + 8, 128:256]
        parts = (jnp.where(odd == 1, odd_part, even_part), jnp.where(odd == 1, even_part, odd_part))
        for h in range(2):
            wide = jnp.concatenate([parts[h], empty], axis=1)
            wide = pltpu.roll(wide, starts[h] & 127, 1)
            lane = pl.multiple_of((starts[h] >> 7) * 128, 128)
            cells[128 * h + 8 * t : 128 * h + 8 * t + 8, pl.ds(lane, 256)] = wide
    phase_high = mm(tables_ref[256:384, 0:128], picks).astype(BF16)
    phase_low = mm(tables_ref[256:384, 128:256], picks).astype(BF16)
    high, low = halves(cells[...])
    out = mm(phase_high, high) + mm(phase_high, low) + mm(phase_low, high)
    out_ref[...] = out.astype(BF16)


def y_kernel(in_ref, table_ref, out_ref, hold):
    data = in_ref[...].astype(F32).T.astype(BF16)
    cos, sin = table_ref[0:NV, :], table_ref[NV : 2 * NV, :]
    table = table_ref[2 * NV : 2 * NV + 128, :]
    high, low = halves(jnp.concatenate([table, turned(table)], axis=1))
    both = mm(data, high) + mm(data, low)
    rows = halves(table_ref[2 * NV + 128 : 2 * NV + 160, 0 : 2 * NV])
    for u in range(NU):
        plain = both[NV * u : NV * (u + 1), 0:128]
        turn = both[NV * u : NV * (u + 1), 128:256]
        lines = jnp.concatenate([plain * cos + turn * sin, turn * cos - plain * sin], axis=0)
        high, low = halves(lines)
        out = mm(rows[0], high) + mm(rows[0], low) + mm(rows[1], high)
        hold[pl.ds(u, 32, stride=NU), :] = out
    out_ref[...] = hold[...].reshape(LINES).astype(BF16)


def rotated(value, cos, sin):
    plain, turn = value
    return plain * cos + turn * sin, turn * cos - plain * sin


def eighths(value, count, sign):
    plain, turn = value
    if count == 0:
        return value
    if count == 2:
        return (turn, -plain) if sign > 0 else (-turn, plain)
    if count == 3:
        return eighths(eighths(value, 2, sign), 1, sign)
    root = math.sqrt(0.5)
    if sign > 0:
        return (plain + turn) * root, (turn - plain) * root
    return (plain - turn) * root, (turn + plain) * root


def short_dft(values, sign):
    count = len(values)
    if count == 1:
        return values
    even, odd = short_dft(values[0::2], sign), short_dft(values[1::2], sign)
    odd = [eighths(value, 8 // count * n, sign) for n, value in enumerate(odd)]
    sums = [(a[0] + b[0], a[1] + b[1]) for a, b in zip(even, odd)]
    return sums + [(a[0] - b[0], a[1] - b[1]) for a, b in zip(even, odd)]


def line_pair(rows, plain, turn):
    four = jnp.concatenate(
        [jnp.concatenate([plain, turn], axis=1), jnp.concatenate([turn, -plain], axis=1)], axis=0
    ).astype(BF16)
    return mm(rows[0], four) + mm(rows[1], four)


def x_kernel(in_ref, real_ref, imag_ref, table_ref, out_ref, hold, hold_turned):
    into = halves(table_ref[0:32, 0:64])
    back = halves(table_ref[32:64, 0:64])
    angles = table_ref[64:96, :]
    second = iota((32, 128), 1) >= 64

    def step(u):
        shape = (32, 128)
        cos, sin = angles[:, u : u + 1], angles[:, NU + u : NU + u + 1]
        return jnp.broadcast_to(cos, shape), jnp.broadcast_to(sin, shape)

    def fold(n):
        n = n + 2 * NU
        return jnp.where(second, angles[:, n : n + 1], 1.0), jnp.where(second, angles[:, n + 8 : n + 9], 0.0)

    data = in_ref[...].astype(F32).reshape(384, 128)
    hold[...] = data
    hold_turned[...] = turned(data)
    classes = [None] * 8
    for u in range(NU):
        plain = hold[pl.ds(u, 32, stride=NU), :]
        both = line_pair(into, plain, hold_turned[pl.ds(u, 32, stride=NU), :])
        value = rotated((both[:, 0:128], both[:, 128:256]), *step(u))
        at = (u - 2) % 8
        classes[at] = value if classes[at] is None else tuple(a + b for a, b in zip(classes[at], value))
    lines = short_dft(classes, 1)

    def wide(green):
        green = green.reshape(32, 512)
        first, second = green[:, 0:256], green[:, 256:512]
        return jnp.concatenate([first, first, second, second], axis=0).T

    real, imag = wide(real_ref[...]), wide(imag_ref[...])
    for n in range(8):
        rows = slice(32 * n, 32 * n + 32)
        cos, sin = fold(n)
        plain, turn = rotated(lines[n], cos, sin)
        plain, turn = crossed(plain), crossed(turn)
        plain, turn = plain * real[rows] - turn * imag[rows], turn * real[rows] + plain * imag[rows]
        lines[n] = rotated((crossed(plain), crossed(turn)), cos, -sin)
    classes = short_dft(lines, -1)
    for u in range(NU):
        cos, sin = step(u)
        value = rotated(classes[(u - 2) % 8], cos, -sin)
        high, low = halves(jnp.concatenate(value, axis=0))
        out = mm(back[0], high) + mm(back[0], low) + mm(back[1], high)
        hold[pl.ds(u, 32, stride=NU), :] = out
    out_ref[...] = hold[...].reshape(LINES).astype(BF16)


def y_back_kernel(in_ref, table_ref, out_ref, hold, hold_turned):
    data = in_ref[...].astype(F32).reshape(384, 128)
    hold[...] = data
    hold_turned[...] = turned(data)
    cos, sin = table_ref[0:NV, :], table_ref[NV : 2 * NV, :]
    tab = halves(table_ref[2 * NV : 2 * NV + 128, :])
    rows = halves(table_ref[2 * NV + 128 : 3 * NV + 128, 0:64])
    lines = []
    for u in range(NU):
        plain = hold[pl.ds(u, 32, stride=NU), :]
        turn = hold_turned[pl.ds(u, 32, stride=NU), :]
        both = line_pair(rows, plain, turn)
        lines.append(both[:, 0:128] * cos - both[:, 128:256] * sin)
    lines.append(jnp.zeros((CELLS - NU * NV, 128), F32))
    high, low = halves(jnp.concatenate(lines, axis=0))
    out = mm_nt(tab[0], high) + mm_nt(tab[0], low) + mm_nt(tab[1], high)
    out_ref[...] = out.astype(BF16)


def node_lanes():
    node = iota((256, 256), 0)
    lane = ((node >> 5) & 1) * 128 + (node >> 6) * NV + ((node >> 2) & 7)
    return jnp.where(iota((256, 256), 1) == lane, 1.0, 0.0).astype(BF16)


def gather_kernel(
    in_ref,
    ints_ref,
    proj_ref,
    slots_ref,
    blocks_ref,
    table_ref,
    out_ref,
    anchor_ref,
    cells,
    patch,
    layers,
    nodes,
    pick,
    near,
    total,
    sem,
):
    copy = pltpu.make_async_copy(ints_ref.at[16:24], anchor_ref, sem)
    copy.start()
    slot = as_row(ints_ref[0 : SOURCES // 128, :])
    pick[...] = slot_picks(slot)
    picks = layer_picks(ints_ref[16:19, 0:TILES])
    tab = halves(table_ref[...])
    phase_high = mm(tab[0], picks).T.astype(BF16)
    phase_low = mm(tab[1], picks).T.astype(BF16)
    data = in_ref[...]
    field = mm(phase_high, data) + mm(phase_low, data)
    cells[...] = field.astype(BF16).astype(F32)
    copy.wait()
    sign = jnp.where(iota((2, 128), 0) == 0, -1.0, 1.0)
    values = []
    for q in range(0, PAIRS, 2):
        lines = []
        for n in (q, q + 1):
            source = slots_ref[pl.ds(anchor_ref[5, n] * 2, 2), :]
            turn = jnp.concatenate([source[1:2], source[0:1]], axis=0) * sign
            lines.append(jnp.concatenate([source, turn], axis=1))
        blocks = jnp.concatenate([side_by_side(blocks_ref.at[q], 0), side_by_side(blocks_ref.at[q + 1], 0)], axis=0)
        value = mm_nt(jnp.concatenate(lines, axis=0).astype(BF16), blocks)
        values.extend((value[0:2, 0:SLOTS], value[2:4, SLOTS:]))
    near[...] = jnp.zeros_like(near)
    for q in range(PAIRS):
        target = pl.ds(anchor_ref[4, q] * 2, 2)
        near[target, :] = near[target, :] + values[q]
    for t in range(TILES):
        odd, starts = place(anchor_ref, t)
        parts = []
        for h in range(2):
            lane = pl.multiple_of((starts[h] >> 7) * 128, 128)
            wide = cells[128 * h + 8 * t : 128 * h + 8 * t + 8, pl.ds(lane, 256)]
            parts.append(pltpu.roll(wide, (256 - (starts[h] & 127)) & 255, 1)[:, 0:128])
        patch[8 * t : 8 * t + 8, 0:128] = jnp.where(odd == 1, parts[1], parts[0])
        patch[8 * t : 8 * t + 8, 128:256] = jnp.where(odd == 1, parts[0], parts[1])
    value = mm_nt(patch[...].astype(BF16), node_lanes())
    layers[0:128, :] = value[:, 0:128]
    layers[128:256, :] = value[:, 128:256]
    layer = iota((32, 128), 1) % 4
    for half in range(2):
        value = layers[pl.ds(128 * half, 32, stride=4), :]
        for b in range(1, 4):
            value = jnp.where(layer == b, layers[pl.ds(128 * half + b, 32, stride=4), :], value)
        nodes[:, 128 * half : 128 * half + 128] = value
    first = iota((4, SLOTS), 0) < 2
    for t in range(0, TILES, 2):
        value = mm(nodes[2 * t : 2 * t + 4, :].astype(BF16), side_by_side(proj_ref, t))
        total[2 * t : 2 * t + 4, :] = jnp.where(first, value[:, 0:SLOTS], value[:, SLOTS:])
    high, low = halves(total[...] + near[...])
    value = mm(high, pick[...]) + mm(low, pick[...])
    value = jnp.where(iota((32, SOURCES), 0) // 2 == (slot >> 7), value, 0.0)
    value = value[0:8] + value[8:16] + value[16:24] + value[24:32]
    value = value + pltpu.roll(value, 4, 0)
    value = value + pltpu.roll(value, 2, 0)
    out_ref[...] = value[0:2]


VM = pl.BlockSpec(memory_space=pltpu.VMEM)
HB = pl.BlockSpec(memory_space=pltpu.HBM)


def call(kernel, outs, in_specs, scratch, flops, moved):
    return pl.pallas_call(
        kernel,
        out_shape=outs,
        in_specs=in_specs,
        out_specs=[VM] * len(outs),
        scratch_shapes=scratch,
        compiler_params=pltpu.CompilerParams(vmem_limit_bytes=VMEM_LIMIT),
        cost_estimate=pl.CostEstimate(flops=flops, bytes_accessed=moved, transcendentals=0),
    )


def shape(*dims, dtype=F32):
    return jax.ShapeDtypeStruct(dims, dtype)


def held(*dims, dtype=F32):
    return pltpu.VMEM(dims, dtype)


def swap(cells, axis):
    parts = lax.axis_size(axis)
    blocks = cells.reshape((parts, -1) + cells.shape[1:] if cells.ndim == 3 else (parts, 8, -1))
    order = ORDER_X if axis == "gx" else ORDER_Y
    moved = lax.all_to_all(blocks, axis, 0, 0, axis_index_groups=[list(order)], tiled=True)
    return moved.reshape(cells.shape)


def body(charges, source_slot, tile_anchor, projection, near_pairs, near_blocks, green_real, green_imag):
    first, z_back = z_tables()
    y_table, y_back = y_tables()
    block = pltpu.VMEM((384, 128), F32)
    cells, slots, ints = call(
        spread_kernel,
        [held(128, CELLS, dtype=BF16), held(32, SLOTS), held(24, 128, dtype=jnp.int32)],
        [HB] * 6,
        [
            pltpu.VMEM((2, SOURCES), F32),
            pltpu.VMEM((SOURCES // 128, 128), jnp.int32),
            pltpu.SMEM((3, TILES), jnp.int32),
            pltpu.VMEM((3, TILES), jnp.int32),
            pltpu.VMEM((2, PAIRS), jnp.int32),
            pltpu.VMEM((TILES, 256, SLOTS), BF16),
            pltpu.VMEM((384, 256), BF16),
            pltpu.VMEM((32, 256), F32),
            pltpu.VMEM((256, 128), F32),
            pltpu.VMEM((128, 256), F32),
            pltpu.VMEM((256, CELLS), F32),
            pltpu.SemaphoreType.DMA((10,)),
        ],
        10**9,
        2 * 10**6,
    )(
        *[
            pltpu.with_memory_space_constraint(array, pltpu.HBM)
            for array in (charges, source_slot.reshape(-1, 128), tile_anchor.T, near_pairs.T, projection, first)
        ]
    )
    cells = swap(cells, "gy")
    line_shape = held(*LINES, dtype=BF16)
    lines = call(y_kernel, [line_shape], [VM] * 2, [block], 10**9, 10**6)(cells, y_table)[0]
    lines = swap(lines, "gx")
    lines = call(x_kernel, [line_shape], [VM] * 4, [block] * 2, 10**9, 10**6)(
        lines, green_real.transpose(1, 2, 0), green_imag.transpose(1, 2, 0), x_tables()
    )[0]
    lines = swap(lines, "gx")
    cells = call(y_back_kernel, [held(128, CELLS, dtype=BF16)], [VM] * 2, [block] * 2, 10**9, 10**6)(lines, y_back)[0]
    cells = swap(cells, "gy")
    return call(
        gather_kernel,
        [shape(2, SOURCES)],
        [VM] * 6,
        [
            pltpu.SMEM((8, 128), jnp.int32),
            pltpu.VMEM((256, CELLS), F32),
            pltpu.VMEM((128, 256), F32),
            pltpu.VMEM((256, 128), F32),
            pltpu.VMEM((32, 256), F32),
            pltpu.VMEM((SLOTS, SOURCES), BF16),
            pltpu.VMEM((32, SLOTS), F32),
            pltpu.VMEM((32, SLOTS), F32),
            pltpu.SemaphoreType.DMA,
        ],
        10**9,
        2 * 10**6,
    )(cells, ints, projection, slots, near_blocks, z_back)[0]


def solution(mesh):
    return jax.shard_map(
        body,
        mesh=mesh,
        in_specs=(
            P(None, ("gx", "gy")),
            P(("gx", "gy")),
            P(("gx", "gy"), None),
            P(("gx", "gy"), None, None),
            P(("gx", "gy"), None),
            P(("gx", "gy"), None, None, None),
            P(None, "gx", "gy"),
            P(None, "gx", "gy"),
        ),
        out_specs=P(None, ("gx", "gy")),
        check_vma=False,
    )
```

```python
import math

import jax
import jax.numpy as jnp
import ml_dtypes
import numpy as np
from jax import lax
from jax.experimental import pallas as pl
from jax.experimental.pallas import tpu as pltpu
from jax.sharding import PartitionSpec as P

TILES = 16
SLOTS = 128
PAIRS = 8
SOURCES = 1536
NU = 12
LINES = (96, 4, 128)
ORDER_X = (1, 10, 19, 14, 6, 7, 15, 13, 18, 20, 24, 0, 11, 31, 5, 30, 4, 3, 26, 2, 9, 21, 22, 29, 23, 28, 8, 27, 12, 17, 16, 25)
ORDER_Y = tuple(2 * z + x for x in range(2) for z in range(8))
NV = 40
CELLS = 512
F32 = jnp.float32
BF16 = jnp.bfloat16
VMEM_LIMIT = 16 * 1024 * 1024


def split_table(table):
    high = table.astype(np.float32).astype(ml_dtypes.bfloat16)
    low = (table - high.astype(np.float64)).astype(np.float32).astype(ml_dtypes.bfloat16)
    return high, low


def as_real(theta, inverse):
    sign = -1.0 if inverse else 1.0
    cos, sin = np.cos(theta), sign * np.sin(theta)
    return np.stack([np.stack([cos, sin], -1), np.stack([-sin, cos], -1)], -2)


def z_tables():
    kz = np.arange(32)
    theta = 2.0 * np.pi * (np.outer(kz, kz) % 32) / 32
    forward = as_real(theta, False).reshape(16, 2, 32, 2, 2)[list(ORDER_Y)]
    table = np.einsum("jqzoc,hg->jhqogcz", forward, np.eye(2)).reshape(128, 128)
    backward = as_real(theta, True).reshape(16, 2, 32, 2, 2)[list(ORDER_Y)] / 32.0
    table_back = np.einsum("jqzoc,hg->jhqcgoz", backward, np.eye(2)).reshape(128, 128)
    first = np.zeros((384, 256), ml_dtypes.bfloat16)
    p = np.arange(256)
    first[p, (p // 32 % 2) * 128 + (p // 64) * NV + p // 4 % 8] = 1.0
    first[256:384, 0:128], first[256:384, 128:256] = split_table(table)
    return jnp.asarray(first), in_rows(table_back)


def in_rows(*tables):
    padded = [np.pad(table, ((0, 0), (0, 128 - table.shape[1]))) for table in tables]
    return jnp.asarray(np.concatenate(padded, 0).astype(np.float32))


def y_tables():
    k = np.arange(16)
    theta = 2.0 * np.pi * (np.outer(k, np.array(ORDER_Y)) % 16) / 16
    eyes = np.einsum("hg,qr->hgqr", np.eye(2), np.eye(2))
    table = np.einsum("kjoc,hgqr->jhqcgokr", as_real(theta, False), eyes).reshape(128, 128)
    table_back = np.einsum("kjoc,hgqr->jgrohckq", as_real(theta, True) / 512.0, eyes).reshape(128, 128)
    phi = 2.0 * np.pi * np.outer(np.arange(NV) - 4, k) / 512
    wide = np.broadcast_to(phi[:, None, None, :, None], (NV, 2, 2, 16, 2)).reshape(NV, 128)
    psi = 2.0 * np.pi * (np.outer(np.array(ORDER_X), np.arange(NV) - 4) % 32) / 32
    rows = np.concatenate([np.cos(psi), np.sin(psi)], 1)
    rows_back = np.concatenate([np.cos(psi.T), -np.sin(psi.T)], 1)
    turn = (np.cos(wide), np.sin(wide))
    return in_rows(*turn, table, rows), in_rows(*turn, table_back, rows_back)


def x_tables():
    k0 = np.arange(32)
    alpha = 2.0 * np.pi * (np.outer(k0, np.array(ORDER_X)) % 32) / 32
    rows = np.concatenate([np.cos(alpha), np.sin(alpha)], 1)
    rows_back = np.concatenate([np.cos(alpha.T), -np.sin(alpha.T)], 1) / 512.0
    beta = 2.0 * np.pi * np.outer(k0, np.arange(NU) - 2) / 256
    phi = 2.0 * np.pi * (k0[:, None] + 32 * np.arange(8)[None, :]) / 512
    return in_rows(rows, rows_back, np.concatenate([np.cos(beta), np.sin(beta), np.cos(phi), np.sin(phi)], 1))


def mm(a, b):
    return lax.dot_general(a, b, (((1,), (0,)), ((), ())), preferred_element_type=F32)


def mm_nt(a, b):
    return lax.dot_general(a, b, (((1,), (1,)), ((), ())), preferred_element_type=F32)


def halves(value):
    high = value.astype(BF16)
    return high, (value - high.astype(F32)).astype(BF16)


def thrice(value, axis):
    high, low = halves(value)
    return jnp.concatenate([high, low, high], axis=axis)


def thrice_other(value, axis):
    high, low = halves(value)
    return jnp.concatenate([high, high, low], axis=axis)


def twice(value, axis):
    return jnp.concatenate([value, value], axis=axis)


def iota(shape, axis):
    return lax.broadcasted_iota(jnp.int32, shape, axis)


def turned(value):
    bit = (iota(value.shape, 1) // 32) % 2
    return jnp.where(bit == 0, pltpu.roll(value, 96, 1), -pltpu.roll(value, 32, 1))


def crossed(value):
    half = iota(value.shape, 1) // 64
    return pltpu.roll(value, 64, 1) + jnp.where(half == 0, value, -value)


def layer_picks(anchor):
    fan = jnp.where(iota((TILES, 256), 0) == (iota((TILES, 256), 1) // 8) % TILES, 1.0, 0.0).astype(BF16)
    low = mm(anchor[2:3, :].astype(F32).astype(BF16), fan)
    at = iota((1, 256), 1)
    want = low + ((at // 128) * 64 + ((at // 4) % 2) * 32 + at % 4).astype(F32)
    return jnp.where(iota((128, 256), 0) == want.astype(jnp.int32), 1.0, 0.0).astype(BF16)


def place(anchor_ref, t):
    x = (anchor_ref[0, t] & 15) + 1
    y = (anchor_ref[1, t] & 31) + 1
    starts = (((x + 1) >> 1) * NV + y, (x >> 1) * NV + y)
    return x & 1, starts


def as_row(slot):
    return jnp.concatenate([slot[r : r + 1, :] for r in range(SOURCES // 128)], axis=1)


def slot_picks(slot):
    return jnp.where(iota((SLOTS, SOURCES), 0) == (slot & 127), 1.0, 0.0).astype(BF16)


def side_by_side(ref, n):
    return jnp.concatenate([ref[n], ref[n + 1]], axis=1)


def spread_kernel(
    charges_hbm,
    slot_hbm,
    anchor_hbm,
    pairs_hbm,
    proj_hbm,
    tables_hbm,
    out_ref,
    slots_ref,
    ints_ref,
    charges_ref,
    slot_ref,
    anchor_ref,
    anchor_vec,
    pairs_vec,
    proj_ref,
    tables_ref,
    nodes,
    layers,
    patch,
    cells,
    sems,
):
    fetched = (
        (charges_hbm, charges_ref),
        (slot_hbm, slot_ref),
        (anchor_hbm, anchor_ref),
        (anchor_hbm, anchor_vec),
        (pairs_hbm, pairs_vec),
    ) + tuple((proj_hbm.at[n : n + 8], proj_ref.at[n : n + 8]) for n in range(0, TILES, 8))
    fetched = fetched + ((tables_hbm, tables_ref),)
    copies = [pltpu.make_async_copy(src, dst, sems.at[n]) for n, (src, dst) in enumerate(fetched)]
    for copy in copies:
        copy.start()
    cells[...] = jnp.zeros_like(cells)
    for copy in copies[:5]:
        copy.wait()
    ints_ref[...] = jnp.zeros_like(ints_ref)
    ints_ref[0 : SOURCES // 128, :] = slot_ref[...]
    ints_ref[16:19, 0:TILES] = anchor_vec[...]
    ints_ref[20:22, 0:PAIRS] = pairs_vec[...]
    slot = as_row(slot_ref[...])
    row = iota((32, SOURCES), 0)
    charge = jnp.where(row % 2 == 0, charges_ref[0:1, :], charges_ref[1:2, :])
    held = jnp.where(row // 2 == (slot >> 7), charge, 0.0).astype(BF16)
    slots_ref[...] = mm_nt(held, slot_picks(slot))
    picks = layer_picks(anchor_vec[...])
    first = iota((4, SLOTS), 0) < 2
    for t in range(0, TILES, 2):
        if t % 8 == 0:
            copies[5 + t // 8].wait()
        mine = slots_ref[2 * t : 2 * t + 4, :]
        mine = jnp.concatenate([jnp.where(first, mine, 0.0), jnp.where(first, 0.0, mine)], axis=1)
        nodes[2 * t : 2 * t + 4, :] = mm_nt(mine.astype(BF16), side_by_side(proj_ref, t))
    value = nodes[...]
    layer = iota((32, 128), 1) % 4
    for half in range(2):
        for b in range(4):
            part = value[:, 128 * half : 128 * half + 128]
            layers[pl.ds(128 * half + b, 32, stride=4), :] = jnp.where(layer == b, part, 0.0)
    high, low = halves(jnp.concatenate([layers[0:128, :], layers[128:256, :]], axis=1))
    copies[7].wait()
    spread = tables_ref[0:256, :]
    patch[...] = mm(high, spread) + mm(low, spread)
    empty = jnp.zeros((8, 128), F32)
    for t in range(TILES):
        odd, starts = place(anchor_ref, t)
        even_part = patch[8 * t : 8 * t + 8, 0:128]
        odd_part = patch[8 * t : 8 * t + 8, 128:256]
        parts = (jnp.where(odd == 1, odd_part, even_part), jnp.where(odd == 1, even_part, odd_part))
        for h in range(2):
            wide = jnp.concatenate([parts[h], empty], axis=1)
            wide = pltpu.roll(wide, starts[h] & 127, 1)
            lane = pl.multiple_of((starts[h] >> 7) * 128, 128)
            cells[128 * h + 8 * t : 128 * h + 8 * t + 8, pl.ds(lane, 256)] = wide
    phase_high = mm(tables_ref[256:384, 0:128], picks).astype(BF16)
    phase_low = mm(tables_ref[256:384, 128:256], picks).astype(BF16)
    high, low = halves(cells[...])
    out = mm(phase_high, high) + mm(phase_high, low) + mm(phase_low, high)
    out_ref[...] = out.astype(BF16)


def y_kernel(in_ref, table_ref, out_ref, hold):
    data = in_ref[...].astype(F32).T.astype(BF16)
    cos, sin = table_ref[0:NV, :], table_ref[NV : 2 * NV, :]
    table = table_ref[2 * NV : 2 * NV + 128, :]
    high, low = halves(jnp.concatenate([table, turned(table)], axis=1))
    both = mm(twice(data, 1), jnp.concatenate([high, low], axis=0))
    rows = thrice_other(table_ref[2 * NV + 128 : 2 * NV + 160, 0 : 2 * NV], 1)
    for u in range(0, NU, 2):
        lines = []
        for n in (u, u + 1):
            plain = both[NV * n : NV * (n + 1), 0:128]
            turn = both[NV * n : NV * (n + 1), 128:256]
            lines.append(jnp.concatenate([plain * cos + turn * sin, turn * cos - plain * sin], axis=0))
        out = mm(rows, thrice(jnp.concatenate(lines, axis=1), 0))
        hold[pl.ds(u, 32, stride=NU), :] = out[:, 0:128]
        hold[pl.ds(u + 1, 32, stride=NU), :] = out[:, 128:256]
    out_ref[...] = hold[...].reshape(LINES).astype(BF16)


def rotated(value, cos, sin):
    plain, turn = value
    return plain * cos + turn * sin, turn * cos - plain * sin


def eighths(value, count, sign):
    plain, turn = value
    if count == 0:
        return value
    if count == 2:
        return (turn, -plain) if sign > 0 else (-turn, plain)
    if count == 3:
        return eighths(eighths(value, 2, sign), 1, sign)
    root = math.sqrt(0.5)
    if sign > 0:
        return (plain + turn) * root, (turn - plain) * root
    return (plain - turn) * root, (turn + plain) * root


def short_dft(values, sign):
    count = len(values)
    if count == 1:
        return values
    even, odd = short_dft(values[0::2], sign), short_dft(values[1::2], sign)
    odd = [eighths(value, 8 // count * n, sign) for n, value in enumerate(odd)]
    sums = [(a[0] + b[0], a[1] + b[1]) for a, b in zip(even, odd)]
    return sums + [(a[0] - b[0], a[1] - b[1]) for a, b in zip(even, odd)]


def line_pair(rows, plain, turn):
    four = jnp.concatenate(
        [jnp.concatenate([plain, turn], axis=1), jnp.concatenate([turn, -plain], axis=1)], axis=0
    ).astype(BF16)
    return mm(rows, twice(four, 0))


def x_kernel(in_ref, real_ref, imag_ref, table_ref, out_ref, hold, hold_turned):
    into = jnp.concatenate(halves(table_ref[0:32, 0:64]), axis=1)
    back = thrice_other(table_ref[32:64, 0:64], 1)
    angles = table_ref[64:96, :]
    second = iota((32, 128), 1) >= 64

    def step(u):
        shape = (32, 128)
        cos, sin = angles[:, u : u + 1], angles[:, NU + u : NU + u + 1]
        return jnp.broadcast_to(cos, shape), jnp.broadcast_to(sin, shape)

    def fold(n):
        n = n + 2 * NU
        return jnp.where(second, angles[:, n : n + 1], 1.0), jnp.where(second, angles[:, n + 8 : n + 9], 0.0)

    data = in_ref[...].astype(F32).reshape(384, 128)
    hold[...] = data
    hold_turned[...] = turned(data)
    classes = [None] * 8
    for u in range(NU):
        plain = hold[pl.ds(u, 32, stride=NU), :]
        both = line_pair(into, plain, hold_turned[pl.ds(u, 32, stride=NU), :])
        value = rotated((both[:, 0:128], both[:, 128:256]), *step(u))
        at = (u - 2) % 8
        classes[at] = value if classes[at] is None else tuple(a + b for a, b in zip(classes[at], value))
    lines = short_dft(classes, 1)

    def wide(green):
        green = green.reshape(32, 512)
        first, second = green[:, 0:256], green[:, 256:512]
        return jnp.concatenate([first, first, second, second], axis=0).T

    real, imag = wide(real_ref[...]), wide(imag_ref[...])
    for n in range(8):
        rows = slice(32 * n, 32 * n + 32)
        cos, sin = fold(n)
        plain, turn = rotated(lines[n], cos, sin)
        plain, turn = crossed(plain), crossed(turn)
        plain, turn = plain * real[rows] - turn * imag[rows], turn * real[rows] + plain * imag[rows]
        lines[n] = rotated((crossed(plain), crossed(turn)), cos, -sin)
    classes = short_dft(lines, -1)
    for u in range(0, NU, 2):
        values = []
        for n in (u, u + 1):
            cos, sin = step(n)
            values.append(jnp.concatenate(rotated(classes[(n - 2) % 8], cos, -sin), axis=0))
        out = mm(back, thrice(jnp.concatenate(values, axis=1), 0))
        hold[pl.ds(u, 32, stride=NU), :] = out[:, 0:128]
        hold[pl.ds(u + 1, 32, stride=NU), :] = out[:, 128:256]
    out_ref[...] = hold[...].reshape(LINES).astype(BF16)


def y_back_kernel(in_ref, table_ref, out_ref, hold, hold_turned):
    data = in_ref[...].astype(F32).reshape(384, 128)
    hold[...] = data
    hold_turned[...] = turned(data)
    cos, sin = table_ref[0:NV, :], table_ref[NV : 2 * NV, :]
    tab = thrice_other(table_ref[2 * NV : 2 * NV + 128, :], 1)
    rows = jnp.concatenate(halves(table_ref[2 * NV + 128 : 3 * NV + 128, 0:64]), axis=1)
    lines = []
    for u in range(NU):
        plain = hold[pl.ds(u, 32, stride=NU), :]
        turn = hold_turned[pl.ds(u, 32, stride=NU), :]
        both = line_pair(rows, plain, turn)
        lines.append(both[:, 0:128] * cos - both[:, 128:256] * sin)
    lines.append(jnp.zeros((CELLS - NU * NV, 128), F32))
    out = mm_nt(tab, thrice(jnp.concatenate(lines, axis=0), 1))
    out_ref[...] = out.astype(BF16)


def node_lanes():
    node = iota((256, 256), 0)
    lane = ((node >> 5) & 1) * 128 + (node >> 6) * NV + ((node >> 2) & 7)
    return jnp.where(iota((256, 256), 1) == lane, 1.0, 0.0).astype(BF16)


def gather_kernel(
    in_ref,
    ints_ref,
    proj_ref,
    slots_ref,
    blocks_ref,
    table_ref,
    out_ref,
    anchor_ref,
    cells,
    patch,
    layers,
    nodes,
    pick,
    near,
    total,
    sem,
):
    copy = pltpu.make_async_copy(ints_ref.at[16:24], anchor_ref, sem)
    copy.start()
    slot = as_row(ints_ref[0 : SOURCES // 128, :])
    pick[...] = slot_picks(slot)
    picks = layer_picks(ints_ref[16:19, 0:TILES])
    tab = halves(table_ref[...])
    phase = mm(jnp.concatenate(tab, axis=0), picks).T.astype(BF16)
    field = mm(phase, twice(in_ref[...], 0))
    cells[...] = field.astype(BF16).astype(F32)
    copy.wait()
    sign = jnp.where(iota((2, 128), 0) == 0, -1.0, 1.0)
    values = []
    for q in range(0, PAIRS, 2):
        lines = []
        for n in (q, q + 1):
            source = slots_ref[pl.ds(anchor_ref[5, n] * 2, 2), :]
            turn = jnp.concatenate([source[1:2], source[0:1]], axis=0) * sign
            lines.append(jnp.concatenate([source, turn], axis=1))
        blocks = jnp.concatenate([side_by_side(blocks_ref.at[q], 0), side_by_side(blocks_ref.at[q + 1], 0)], axis=0)
        value = mm_nt(jnp.concatenate(lines, axis=0).astype(BF16), blocks)
        values.extend((value[0:2, 0:SLOTS], value[2:4, SLOTS:]))
    near[...] = jnp.zeros_like(near)
    for q in range(PAIRS):
        target = pl.ds(anchor_ref[4, q] * 2, 2)
        near[target, :] = near[target, :] + values[q]
    for t in range(TILES):
        odd, starts = place(anchor_ref, t)
        parts = []
        for h in range(2):
            lane = pl.multiple_of((starts[h] >> 7) * 128, 128)
            wide = cells[128 * h + 8 * t : 128 * h + 8 * t + 8, pl.ds(lane, 256)]
            parts.append(pltpu.roll(wide, (256 - (starts[h] & 127)) & 255, 1)[:, 0:128])
        patch[8 * t : 8 * t + 8, 0:128] = jnp.where(odd == 1, parts[1], parts[0])
        patch[8 * t : 8 * t + 8, 128:256] = jnp.where(odd == 1, parts[0], parts[1])
    value = mm_nt(patch[...].astype(BF16), node_lanes())
    layers[0:128, :] = value[:, 0:128]
    layers[128:256, :] = value[:, 128:256]
    layer = iota((32, 128), 1) % 4
    for half in range(2):
        value = layers[pl.ds(128 * half, 32, stride=4), :]
        for b in range(1, 4):
            value = jnp.where(layer == b, layers[pl.ds(128 * half + b, 32, stride=4), :], value)
        nodes[:, 128 * half : 128 * half + 128] = value
    first = iota((4, SLOTS), 0) < 2
    for t in range(0, TILES, 2):
        value = mm(nodes[2 * t : 2 * t + 4, :].astype(BF16), side_by_side(proj_ref, t))
        total[2 * t : 2 * t + 4, :] = jnp.where(first, value[:, 0:SLOTS], value[:, SLOTS:])
    value = mm(jnp.concatenate(halves(total[...] + near[...]), axis=1), twice(pick[...], 0))
    value = jnp.where(iota((32, SOURCES), 0) // 2 == (slot >> 7), value, 0.0)
    value = value[0:8] + value[8:16] + value[16:24] + value[24:32]
    value = value + pltpu.roll(value, 4, 0)
    value = value + pltpu.roll(value, 2, 0)
    out_ref[...] = value[0:2]


VM = pl.BlockSpec(memory_space=pltpu.VMEM)
HB = pl.BlockSpec(memory_space=pltpu.HBM)


def call(kernel, outs, in_specs, scratch, flops, moved):
    return pl.pallas_call(
        kernel,
        out_shape=outs,
        in_specs=in_specs,
        out_specs=[VM] * len(outs),
        scratch_shapes=scratch,
        compiler_params=pltpu.CompilerParams(vmem_limit_bytes=VMEM_LIMIT),
        cost_estimate=pl.CostEstimate(flops=flops, bytes_accessed=moved, transcendentals=0),
    )


def shape(*dims, dtype=F32):
    return jax.ShapeDtypeStruct(dims, dtype)


def held(*dims, dtype=F32):
    return pltpu.VMEM(dims, dtype)


def swap(cells, axis):
    parts = lax.axis_size(axis)
    blocks = cells.reshape((parts, -1) + cells.shape[1:] if cells.ndim == 3 else (parts, 8, -1))
    order = ORDER_X if axis == "gx" else ORDER_Y
    moved = lax.all_to_all(blocks, axis, 0, 0, axis_index_groups=[list(order)], tiled=True)
    return moved.reshape(cells.shape)


def body(charges, source_slot, tile_anchor, projection, near_pairs, near_blocks, green_real, green_imag):
    first, z_back = z_tables()
    y_table, y_back = y_tables()
    block = pltpu.VMEM((384, 128), F32)
    cells, slots, ints = call(
        spread_kernel,
        [held(128, CELLS, dtype=BF16), held(32, SLOTS), held(24, 128, dtype=jnp.int32)],
        [HB] * 6,
        [
            pltpu.VMEM((2, SOURCES), F32),
            pltpu.VMEM((SOURCES // 128, 128), jnp.int32),
            pltpu.SMEM((3, TILES), jnp.int32),
            pltpu.VMEM((3, TILES), jnp.int32),
            pltpu.VMEM((2, PAIRS), jnp.int32),
            pltpu.VMEM((TILES, 256, SLOTS), BF16),
            pltpu.VMEM((384, 256), BF16),
            pltpu.VMEM((32, 256), F32),
            pltpu.VMEM((256, 128), F32),
            pltpu.VMEM((128, 256), F32),
            pltpu.VMEM((256, CELLS), F32),
            pltpu.SemaphoreType.DMA((8,)),
        ],
        10**9,
        2 * 10**6,
    )(
        *[
            pltpu.with_memory_space_constraint(array, pltpu.HBM)
            for array in (charges, source_slot.reshape(-1, 128), tile_anchor.T, near_pairs.T, projection, first)
        ]
    )
    cells = swap(cells, "gy")
    line_shape = held(*LINES, dtype=BF16)
    lines = call(y_kernel, [line_shape], [VM] * 2, [block], 10**9, 10**6)(cells, y_table)[0]
    lines = swap(lines, "gx")
    lines = call(x_kernel, [line_shape], [VM] * 4, [block] * 2, 10**9, 10**6)(
        lines, green_real.transpose(1, 2, 0), green_imag.transpose(1, 2, 0), x_tables()
    )[0]
    lines = swap(lines, "gx")
    cells = call(y_back_kernel, [held(128, CELLS, dtype=BF16)], [VM] * 2, [block] * 2, 10**9, 10**6)(lines, y_back)[0]
    cells = swap(cells, "gy")
    return call(
        gather_kernel,
        [shape(2, SOURCES)],
        [VM] * 6,
        [
            pltpu.SMEM((8, 128), jnp.int32),
            pltpu.VMEM((256, CELLS), F32),
            pltpu.VMEM((128, 256), F32),
            pltpu.VMEM((256, 128), F32),
            pltpu.VMEM((32, 256), F32),
            pltpu.VMEM((SLOTS, SOURCES), BF16),
            pltpu.VMEM((32, SLOTS), F32),
            pltpu.VMEM((32, SLOTS), F32),
            pltpu.SemaphoreType.DMA,
        ],
        10**9,
        2 * 10**6,
    )(cells, ints, projection, slots, near_blocks, z_back)[0]


def solution(mesh):
    return jax.shard_map(
        body,
        mesh=mesh,
        in_specs=(
            P(None, ("gx", "gy")),
            P(("gx", "gy")),
            P(("gx", "gy"), None),
            P(("gx", "gy"), None, None),
            P(("gx", "gy"), None),
            P(("gx", "gy"), None, None, None),
            P(None, "gx", "gy"),
            P(None, "gx", "gy"),
        ),
        out_specs=P(None, ("gx", "gy")),
        check_vma=False,
    )
```

```python
import math

import jax
import jax.numpy as jnp
import ml_dtypes
import numpy as np
from jax import lax
from jax.experimental import pallas as pl
from jax.experimental.pallas import tpu as pltpu
from jax.sharding import PartitionSpec as P

TILES = 16
SLOTS = 128
PAIRS = 8
SOURCES = 1536
NU = 12
LINES = (96, 4, 128)
ROWS = 384
ORDER_X = (24, 27, 4, 12, 25, 10, 26, 19, 28, 1, 11, 6, 17, 14, 23, 16, 13, 20, 0, 5, 30, 8, 2, 21, 31, 29, 3, 22, 7, 15, 9, 18)
ORDER_Y = tuple(2 * z + x for x in range(2) for z in range(8))
NV = 40
CELLS = 512
F32 = jnp.float32
BF16 = jnp.bfloat16
VMEM_LIMIT = 16 * 1024 * 1024


def split_table(table):
    high = table.astype(np.float32).astype(ml_dtypes.bfloat16)
    low = (table - high.astype(np.float64)).astype(np.float32).astype(ml_dtypes.bfloat16)
    return high, low


def as_real(theta, inverse):
    sign = -1.0 if inverse else 1.0
    cos, sin = np.cos(theta), sign * np.sin(theta)
    return np.stack([np.stack([cos, sin], -1), np.stack([-sin, cos], -1)], -2)


def z_tables():
    kz = np.arange(32)
    theta = 2.0 * np.pi * (np.outer(kz, kz) % 32) / 32
    forward = as_real(theta, False).reshape(16, 2, 32, 2, 2)[list(ORDER_Y)]
    table = np.einsum("jqzoc,hg->jhqogcz", forward, np.eye(2)).reshape(128, 128)
    backward = as_real(theta, True).reshape(16, 2, 32, 2, 2)[list(ORDER_Y)] / 32.0
    table_back = np.einsum("jqzoc,hg->jhqcgoz", backward, np.eye(2)).reshape(128, 128)
    first = np.zeros((384, 256), ml_dtypes.bfloat16)
    p = np.arange(256)
    first[p, (p // 32 % 2) * 128 + (p // 64) * NV + p // 4 % 8] = 1.0
    first[256:384, 0:128], first[256:384, 128:256] = split_table(table)
    return jnp.asarray(first), in_rows(table_back)


def in_rows(*tables):
    padded = [np.pad(table, ((0, 0), (0, 128 - table.shape[1]))) for table in tables]
    return jnp.asarray(np.concatenate(padded, 0).astype(np.float32))


def y_tables():
    k = np.arange(16)
    theta = 2.0 * np.pi * (np.outer(k, np.array(ORDER_Y)) % 16) / 16
    eyes = np.einsum("hg,qr->hgqr", np.eye(2), np.eye(2))
    table = np.einsum("kjoc,hgqr->jhqcgokr", as_real(theta, False), eyes).reshape(128, 128)
    table_back = np.einsum("kjoc,hgqr->jgrohckq", as_real(theta, True) / 512.0, eyes).reshape(128, 128)
    phi = 2.0 * np.pi * np.outer(np.arange(NV) - 4, k) / 512
    wide = np.broadcast_to(phi[:, None, None, :, None], (NV, 2, 2, 16, 2)).reshape(NV, 128)
    psi = 2.0 * np.pi * (np.outer(np.array(ORDER_X), np.arange(NV) - 4) % 32) / 32
    rows = np.concatenate([np.cos(psi), np.sin(psi)], 1)
    rows_back = np.concatenate([np.cos(psi.T), -np.sin(psi.T)], 1)
    turn = (np.cos(wide), np.sin(wide))
    return in_rows(*turn, table, rows), in_rows(*turn, table_back, rows_back)


def x_tables():
    k0 = np.arange(32)
    alpha = 2.0 * np.pi * (np.outer(k0, np.array(ORDER_X)) % 32) / 32
    rows = np.concatenate([np.cos(alpha), np.sin(alpha)], 1)
    rows_back = np.concatenate([np.cos(alpha.T), -np.sin(alpha.T)], 1) / 512.0
    beta = 2.0 * np.pi * np.outer(k0, np.arange(NU) - 2) / 256
    phi = 2.0 * np.pi * (k0[:, None] + 32 * np.arange(8)[None, :]) / 512
    return in_rows(rows, rows_back, np.concatenate([np.cos(beta), np.sin(beta), np.cos(phi), np.sin(phi)], 1))


def mm(a, b):
    return lax.dot_general(a, b, (((1,), (0,)), ((), ())), preferred_element_type=F32)


def mm_nt(a, b):
    return lax.dot_general(a, b, (((1,), (1,)), ((), ())), preferred_element_type=F32)


def halves(value):
    high = value.astype(BF16)
    return high, (value - high.astype(F32)).astype(BF16)


def thrice(value, axis):
    high, low = halves(value)
    return jnp.concatenate([high, low, high], axis=axis)


def thrice_other(value, axis):
    high, low = halves(value)
    return jnp.concatenate([high, high, low], axis=axis)


def twice(value, axis):
    return jnp.concatenate([value, value], axis=axis)


def iota(shape, axis):
    return lax.broadcasted_iota(jnp.int32, shape, axis)


def turned(value):
    bit = (iota(value.shape, 1) // 32) % 2
    return jnp.where(bit == 0, pltpu.roll(value, 96, 1), -pltpu.roll(value, 32, 1))


def crossed(value):
    half = iota(value.shape, 1) // 64
    return pltpu.roll(value, 64, 1) + jnp.where(half == 0, value, -value)


def layer_picks(anchor):
    fan = jnp.where(iota((TILES, 256), 0) == (iota((TILES, 256), 1) // 8) % TILES, 1.0, 0.0).astype(BF16)
    low = mm(anchor[2:3, :].astype(F32).astype(BF16), fan)
    at = iota((1, 256), 1)
    want = low + ((at // 128) * 64 + ((at // 4) % 2) * 32 + at % 4).astype(F32)
    return jnp.where(iota((128, 256), 0) == want.astype(jnp.int32), 1.0, 0.0).astype(BF16)


def place(anchor_ref, t):
    x = (anchor_ref[0, t] & 15) + 1
    y = (anchor_ref[1, t] & 31) + 1
    starts = (((x + 1) >> 1) * NV + y, (x >> 1) * NV + y)
    return x & 1, starts


def as_row(slot):
    return jnp.concatenate([slot[r : r + 1, :] for r in range(SOURCES // 128)], axis=1)


def slot_picks(slot):
    return jnp.where(iota((SLOTS, SOURCES), 0) == (slot & 127), 1.0, 0.0).astype(BF16)


def side_by_side(ref, n):
    return jnp.concatenate([ref[n], ref[n + 1]], axis=1)


def spread_kernel(
    charges_hbm,
    slot_hbm,
    anchor_hbm,
    pairs_hbm,
    proj_hbm,
    tables_hbm,
    out_ref,
    slots_ref,
    ints_ref,
    charges_ref,
    slot_ref,
    anchor_ref,
    anchor_vec,
    pairs_vec,
    proj_ref,
    tables_ref,
    nodes,
    layers,
    patch,
    cells,
    sems,
):
    fetched = (
        (charges_hbm, charges_ref),
        (slot_hbm, slot_ref),
        (anchor_hbm, anchor_ref),
        (anchor_hbm, anchor_vec),
        (pairs_hbm, pairs_vec),
    ) + tuple((proj_hbm.at[n : n + 8], proj_ref.at[n : n + 8]) for n in range(0, TILES, 8))
    fetched = fetched + ((tables_hbm, tables_ref),)
    copies = [pltpu.make_async_copy(src, dst, sems.at[n]) for n, (src, dst) in enumerate(fetched)]
    for copy in copies:
        copy.start()
    cells[...] = jnp.zeros_like(cells)
    for copy in copies[:5]:
        copy.wait()
    ints_ref[...] = jnp.zeros_like(ints_ref)
    ints_ref[0 : SOURCES // 128, :] = slot_ref[...]
    ints_ref[16:19, 0:TILES] = anchor_vec[...]
    ints_ref[20:22, 0:PAIRS] = pairs_vec[...]
    slot = as_row(slot_ref[...])
    row = iota((32, SOURCES), 0)
    charge = jnp.where(row % 2 == 0, charges_ref[0:1, :], charges_ref[1:2, :])
    held = jnp.where(row // 2 == (slot >> 7), charge, 0.0).astype(BF16)
    slots_ref[...] = mm_nt(held, slot_picks(slot))
    picks = layer_picks(anchor_vec[...])
    first = iota((4, SLOTS), 0) < 2
    for t in range(0, TILES, 2):
        if t % 8 == 0:
            copies[5 + t // 8].wait()
        mine = slots_ref[2 * t : 2 * t + 4, :]
        mine = jnp.concatenate([jnp.where(first, mine, 0.0), jnp.where(first, 0.0, mine)], axis=1)
        nodes[2 * t : 2 * t + 4, :] = mm_nt(mine.astype(BF16), side_by_side(proj_ref, t))
    value = nodes[...]
    layer = iota((32, 128), 1) % 4
    for half in range(2):
        for b in range(4):
            part = value[:, 128 * half : 128 * half + 128]
            layers[pl.ds(128 * half + b, 32, stride=4), :] = jnp.where(layer == b, part, 0.0)
    high, low = halves(jnp.concatenate([layers[0:128, :], layers[128:256, :]], axis=1))
    copies[7].wait()
    spread = tables_ref[0:256, :]
    patch[...] = mm(high, spread) + mm(low, spread)
    empty = jnp.zeros((8, 128), F32)
    for t in range(TILES):
        odd, starts = place(anchor_ref, t)
        even_part = patch[8 * t : 8 * t + 8, 0:128]
        odd_part = patch[8 * t : 8 * t + 8, 128:256]
        parts = (jnp.where(odd == 1, odd_part, even_part), jnp.where(odd == 1, even_part, odd_part))
        for h in range(2):
            wide = jnp.concatenate([parts[h], empty], axis=1)
            wide = pltpu.roll(wide, starts[h] & 127, 1)
            lane = pl.multiple_of((starts[h] >> 7) * 128, 128)
            cells[128 * h + 8 * t : 128 * h + 8 * t + 8, pl.ds(lane, 256)] = wide
    phase_high = mm(tables_ref[256:384, 0:128], picks).astype(BF16)
    phase_low = mm(tables_ref[256:384, 128:256], picks).astype(BF16)
    high, low = halves(cells[...])
    out = mm(phase_high, high) + mm(phase_high, low) + mm(phase_low, high)
    out_ref[...] = out.astype(BF16)


def y_kernel(in_ref, table_ref, out_ref, hold):
    data = in_ref[...].astype(F32).T.astype(BF16)
    cos, sin = table_ref[0:NV, :], table_ref[NV : 2 * NV, :]
    table = table_ref[2 * NV : 2 * NV + 128, :]
    high, low = halves(jnp.concatenate([table, turned(table)], axis=1))
    both = mm(twice(data, 1), jnp.concatenate([high, low], axis=0))
    rows = thrice_other(table_ref[2 * NV + 128 : 2 * NV + 160, 0 : 2 * NV], 1)
    for u in range(0, NU, 2):
        lines = []
        for n in (u, u + 1):
            plain = both[NV * n : NV * (n + 1), 0:128]
            turn = both[NV * n : NV * (n + 1), 128:256]
            lines.append(jnp.concatenate([plain * cos + turn * sin, turn * cos - plain * sin], axis=0))
        out = mm(rows, thrice(jnp.concatenate(lines, axis=1), 0))
        hold[pl.ds(u, 32, stride=NU), :] = out[:, 0:128]
        hold[pl.ds(u + 1, 32, stride=NU), :] = out[:, 128:256]
    out_ref[...] = hold[0:ROWS, :].reshape(LINES).astype(BF16)


def rotated(value, cos, sin):
    plain, turn = value
    return plain * cos + turn * sin, turn * cos - plain * sin


def eighths(value, count, sign):
    plain, turn = value
    if count == 0:
        return value
    if count == 2:
        return (turn, -plain) if sign > 0 else (-turn, plain)
    if count == 3:
        return eighths(eighths(value, 2, sign), 1, sign)
    root = math.sqrt(0.5)
    if sign > 0:
        return (plain + turn) * root, (turn - plain) * root
    return (plain - turn) * root, (turn + plain) * root


def short_dft(values, sign):
    count = len(values)
    if count == 1:
        return values
    even, odd = short_dft(values[0::2], sign), short_dft(values[1::2], sign)
    odd = [eighths(value, 8 // count * n, sign) for n, value in enumerate(odd)]
    sums = [(a[0] + b[0], a[1] + b[1]) for a, b in zip(even, odd)]
    return sums + [(a[0] - b[0], a[1] - b[1]) for a, b in zip(even, odd)]


def line_pair(rows, plain, turn):
    four = jnp.concatenate(
        [jnp.concatenate([plain, turn], axis=1), jnp.concatenate([turn, -plain], axis=1)], axis=0
    ).astype(BF16)
    return mm(rows, twice(four, 0))


def x_kernel(in_ref, real_ref, imag_ref, table_ref, out_ref, hold, hold_turned):
    into = jnp.concatenate(halves(table_ref[0:32, 0:64]), axis=1)
    back = thrice_other(table_ref[32:64, 0:64], 1)
    angles = table_ref[64:96, :]
    second = iota((32, 128), 1) >= 64

    def step(u):
        shape = (32, 128)
        cos, sin = angles[:, u : u + 1], angles[:, NU + u : NU + u + 1]
        return jnp.broadcast_to(cos, shape), jnp.broadcast_to(sin, shape)

    def fold(n):
        n = n + 2 * NU
        return jnp.where(second, angles[:, n : n + 1], 1.0), jnp.where(second, angles[:, n + 8 : n + 9], 0.0)

    data = in_ref[...].astype(F32).reshape(ROWS, 128)
    hold[0:ROWS, :] = data
    hold_turned[0:ROWS, :] = turned(data)
    classes = [None] * 8
    for u in range(NU):
        plain = hold[pl.ds(u, 32, stride=NU), :]
        both = line_pair(into, plain, hold_turned[pl.ds(u, 32, stride=NU), :])
        value = rotated((both[:, 0:128], both[:, 128:256]), *step(u))
        at = (u - 2) % 8
        classes[at] = value if classes[at] is None else tuple(a + b for a, b in zip(classes[at], value))
    lines = short_dft(classes, 1)

    def wide(green):
        green = green.reshape(32, 512)
        first, second = green[:, 0:256], green[:, 256:512]
        return jnp.concatenate([first, first, second, second], axis=0).T

    real, imag = wide(real_ref[...]), wide(imag_ref[...])
    for n in range(8):
        rows = slice(32 * n, 32 * n + 32)
        cos, sin = fold(n)
        plain, turn = rotated(lines[n], cos, sin)
        plain, turn = crossed(plain), crossed(turn)
        plain, turn = plain * real[rows] - turn * imag[rows], turn * real[rows] + plain * imag[rows]
        lines[n] = rotated((crossed(plain), crossed(turn)), cos, -sin)
    classes = short_dft(lines, -1)
    for u in range(0, NU, 2):
        values = []
        for n in (u, u + 1):
            cos, sin = step(n)
            values.append(jnp.concatenate(rotated(classes[(n - 2) % 8], cos, -sin), axis=0))
        out = mm(back, thrice(jnp.concatenate(values, axis=1), 0))
        hold[pl.ds(u, 32, stride=NU), :] = out[:, 0:128]
        hold[pl.ds(u + 1, 32, stride=NU), :] = out[:, 128:256]
    out_ref[...] = hold[0:ROWS, :].reshape(LINES).astype(BF16)


def y_back_kernel(in_ref, table_ref, out_ref, hold, hold_turned):
    data = in_ref[...].astype(F32).reshape(ROWS, 128)
    hold[0:ROWS, :] = data
    hold_turned[0:ROWS, :] = turned(data)
    cos, sin = table_ref[0:NV, :], table_ref[NV : 2 * NV, :]
    tab = thrice_other(table_ref[2 * NV : 2 * NV + 128, :], 1)
    rows = jnp.concatenate(halves(table_ref[2 * NV + 128 : 3 * NV + 128, 0:64]), axis=1)
    lines = []
    for u in range(NU):
        plain = hold[pl.ds(u, 32, stride=NU), :]
        turn = hold_turned[pl.ds(u, 32, stride=NU), :]
        both = line_pair(rows, plain, turn)
        lines.append(both[:, 0:128] * cos - both[:, 128:256] * sin)
    lines.append(jnp.zeros((CELLS - NU * NV, 128), F32))
    out = mm_nt(tab, thrice(jnp.concatenate(lines, axis=0), 1))
    out_ref[...] = out.astype(BF16)


def node_lanes():
    node = iota((256, 256), 0)
    lane = ((node >> 5) & 1) * 128 + (node >> 6) * NV + ((node >> 2) & 7)
    return jnp.where(iota((256, 256), 1) == lane, 1.0, 0.0).astype(BF16)


def gather_kernel(
    in_ref,
    ints_ref,
    proj_ref,
    slots_ref,
    blocks_ref,
    table_ref,
    out_ref,
    anchor_ref,
    cells,
    patch,
    layers,
    nodes,
    pick,
    near,
    total,
    sem,
):
    copy = pltpu.make_async_copy(ints_ref.at[16:24], anchor_ref, sem)
    copy.start()
    slot = as_row(ints_ref[0 : SOURCES // 128, :])
    pick[...] = slot_picks(slot)
    picks = layer_picks(ints_ref[16:19, 0:TILES])
    tab = halves(table_ref[...])
    phase = mm(jnp.concatenate(tab, axis=0), picks).T.astype(BF16)
    field = mm(phase, twice(in_ref[...], 0))
    cells[...] = field.astype(BF16).astype(F32)
    copy.wait()
    sign = jnp.where(iota((2, 128), 0) == 0, -1.0, 1.0)
    values = []
    for q in range(0, PAIRS, 2):
        lines = []
        for n in (q, q + 1):
            source = slots_ref[pl.ds(anchor_ref[5, n] * 2, 2), :]
            turn = jnp.concatenate([source[1:2], source[0:1]], axis=0) * sign
            lines.append(jnp.concatenate([source, turn], axis=1))
        blocks = jnp.concatenate([side_by_side(blocks_ref.at[q], 0), side_by_side(blocks_ref.at[q + 1], 0)], axis=0)
        value = mm_nt(jnp.concatenate(lines, axis=0).astype(BF16), blocks)
        values.extend((value[0:2, 0:SLOTS], value[2:4, SLOTS:]))
    near[...] = jnp.zeros_like(near)
    for q in range(PAIRS):
        target = pl.ds(anchor_ref[4, q] * 2, 2)
        near[target, :] = near[target, :] + values[q]
    for t in range(TILES):
        odd, starts = place(anchor_ref, t)
        parts = []
        for h in range(2):
            lane = pl.multiple_of((starts[h] >> 7) * 128, 128)
            wide = cells[128 * h + 8 * t : 128 * h + 8 * t + 8, pl.ds(lane, 256)]
            parts.append(pltpu.roll(wide, (256 - (starts[h] & 127)) & 255, 1)[:, 0:128])
        patch[8 * t : 8 * t + 8, 0:128] = jnp.where(odd == 1, parts[1], parts[0])
        patch[8 * t : 8 * t + 8, 128:256] = jnp.where(odd == 1, parts[0], parts[1])
    value = mm_nt(patch[...].astype(BF16), node_lanes())
    layers[0:128, :] = value[:, 0:128]
    layers[128:256, :] = value[:, 128:256]
    layer = iota((32, 128), 1) % 4
    for half in range(2):
        value = layers[pl.ds(128 * half, 32, stride=4), :]
        for b in range(1, 4):
            value = jnp.where(layer == b, layers[pl.ds(128 * half + b, 32, stride=4), :], value)
        nodes[:, 128 * half : 128 * half + 128] = value
    first = iota((4, SLOTS), 0) < 2
    for t in range(0, TILES, 2):
        value = mm(nodes[2 * t : 2 * t + 4, :].astype(BF16), side_by_side(proj_ref, t))
        total[2 * t : 2 * t + 4, :] = jnp.where(first, value[:, 0:SLOTS], value[:, SLOTS:])
    value = mm(jnp.concatenate(halves(total[...] + near[...]), axis=1), twice(pick[...], 0))
    value = jnp.where(iota((32, SOURCES), 0) // 2 == (slot >> 7), value, 0.0)
    value = value[0:8] + value[8:16] + value[16:24] + value[24:32]
    value = value + pltpu.roll(value, 4, 0)
    value = value + pltpu.roll(value, 2, 0)
    out_ref[...] = value[0:2]


VM = pl.BlockSpec(memory_space=pltpu.VMEM)
HB = pl.BlockSpec(memory_space=pltpu.HBM)


def call(kernel, outs, in_specs, scratch, flops, moved):
    return pl.pallas_call(
        kernel,
        out_shape=outs,
        in_specs=in_specs,
        out_specs=[VM] * len(outs),
        scratch_shapes=scratch,
        compiler_params=pltpu.CompilerParams(vmem_limit_bytes=VMEM_LIMIT),
        cost_estimate=pl.CostEstimate(flops=flops, bytes_accessed=moved, transcendentals=0),
    )


def shape(*dims, dtype=F32):
    return jax.ShapeDtypeStruct(dims, dtype)


def held(*dims, dtype=F32):
    return pltpu.VMEM(dims, dtype)


def swap(cells, axis):
    parts = lax.axis_size(axis)
    blocks = cells.reshape((parts, -1) + cells.shape[1:] if cells.ndim == 3 else (parts, 8, -1))
    order = ORDER_X if axis == "gx" else ORDER_Y
    moved = lax.all_to_all(blocks, axis, 0, 0, axis_index_groups=[list(order)], tiled=True)
    return moved.reshape(cells.shape)


def body(charges, source_slot, tile_anchor, projection, near_pairs, near_blocks, green_real, green_imag):
    first, z_back = z_tables()
    y_table, y_back = y_tables()
    block = pltpu.VMEM((ROWS + 16, 128), F32)
    cells, slots, ints = call(
        spread_kernel,
        [held(128, CELLS, dtype=BF16), held(32, SLOTS), held(24, 128, dtype=jnp.int32)],
        [HB] * 6,
        [
            pltpu.VMEM((2, SOURCES), F32),
            pltpu.VMEM((SOURCES // 128, 128), jnp.int32),
            pltpu.SMEM((3, TILES), jnp.int32),
            pltpu.VMEM((3, TILES), jnp.int32),
            pltpu.VMEM((2, PAIRS), jnp.int32),
            pltpu.VMEM((TILES, 256, SLOTS), BF16),
            pltpu.VMEM((384, 256), BF16),
            pltpu.VMEM((32, 256), F32),
            pltpu.VMEM((264, 128), F32),
            pltpu.VMEM((128, 256), F32),
            pltpu.VMEM((256, CELLS), F32),
            pltpu.SemaphoreType.DMA((8,)),
        ],
        10**9,
        2 * 10**6,
    )(
        *[
            pltpu.with_memory_space_constraint(array, pltpu.HBM)
            for array in (charges, source_slot.reshape(-1, 128), tile_anchor.T, near_pairs.T, projection, first)
        ]
    )
    cells = swap(cells, "gy")
    line_shape = held(*LINES, dtype=BF16)
    lines = call(y_kernel, [line_shape], [VM] * 2, [block], 10**9, 10**6)(cells, y_table)[0]
    lines = swap(lines, "gx")
    lines = call(x_kernel, [line_shape], [VM] * 4, [block] * 2, 10**9, 10**6)(
        lines, green_real.transpose(1, 2, 0), green_imag.transpose(1, 2, 0), x_tables()
    )[0]
    lines = swap(lines, "gx")
    cells = call(y_back_kernel, [held(128, CELLS, dtype=BF16)], [VM] * 2, [block] * 2, 10**9, 10**6)(lines, y_back)[0]
    cells = swap(cells, "gy")
    return call(
        gather_kernel,
        [shape(2, SOURCES)],
        [VM] * 6,
        [
            pltpu.SMEM((8, 128), jnp.int32),
            pltpu.VMEM((256, CELLS), F32),
            pltpu.VMEM((128, 256), F32),
            pltpu.VMEM((264, 128), F32),
            pltpu.VMEM((32, 256), F32),
            pltpu.VMEM((SLOTS, SOURCES), BF16),
            pltpu.VMEM((32, SLOTS), F32),
            pltpu.VMEM((32, SLOTS), F32),
            pltpu.SemaphoreType.DMA,
        ],
        10**9,
        2 * 10**6,
    )(cells, ints, projection, slots, near_blocks, z_back)[0]


def solution(mesh):
    return jax.shard_map(
        body,
        mesh=mesh,
        in_specs=(
            P(None, ("gx", "gy")),
            P(("gx", "gy")),
            P(("gx", "gy"), None),
            P(("gx", "gy"), None, None),
            P(("gx", "gy"), None),
            P(("gx", "gy"), None, None, None),
            P(None, "gx", "gy"),
            P(None, "gx", "gy"),
        ),
        out_specs=P(None, ("gx", "gy")),
        check_vma=False,
    )
```

```python
import math

import jax
import jax.numpy as jnp
import ml_dtypes
import numpy as np
from jax import lax
from jax.experimental import pallas as pl
from jax.experimental.pallas import tpu as pltpu
from jax.sharding import PartitionSpec as P

TILES = 16
SLOTS = 128
PAIRS = 8
SOURCES = 1536
NU = 12
LINES = (96, 4, 128)
ROWS = 384
ORDER_X = (11, 17, 7, 6, 3, 26, 22, 28, 13, 1, 29, 4, 15, 5, 21, 10, 12, 2, 20, 31, 18, 23, 16, 14, 25, 9, 30, 0, 8, 24, 19, 27)
ORDER_Y = tuple(2 * z + x for x in range(2) for z in range(8))
NV = 40
CELLS = 512
F32 = jnp.float32
BF16 = jnp.bfloat16
VMEM_LIMIT = 16 * 1024 * 1024


def split_table(table):
    high = table.astype(np.float32).astype(ml_dtypes.bfloat16)
    low = (table - high.astype(np.float64)).astype(np.float32).astype(ml_dtypes.bfloat16)
    return high, low


def as_real(theta, inverse):
    sign = -1.0 if inverse else 1.0
    cos, sin = np.cos(theta), sign * np.sin(theta)
    return np.stack([np.stack([cos, sin], -1), np.stack([-sin, cos], -1)], -2)


def z_tables():
    kz = np.arange(32)
    theta = 2.0 * np.pi * (np.outer(kz, kz) % 32) / 32
    forward = as_real(theta, False).reshape(16, 2, 32, 2, 2)[list(ORDER_Y)]
    table = np.einsum("jqzoc,hg->jhqogcz", forward, np.eye(2)).reshape(128, 128)
    backward = as_real(theta, True).reshape(16, 2, 32, 2, 2)[list(ORDER_Y)] / 32.0
    table_back = np.einsum("jqzoc,hg->jhqcgoz", backward, np.eye(2)).reshape(128, 128)
    first = np.zeros((384, 256), ml_dtypes.bfloat16)
    p = np.arange(256)
    first[p, (p // 32 % 2) * 128 + (p // 64) * NV + p // 4 % 8] = 1.0
    first[256:384, 0:128], first[256:384, 128:256] = split_table(table)
    return jnp.asarray(first), in_rows(table_back)


def in_rows(*tables):
    padded = [np.pad(table, ((0, 0), (0, 128 - table.shape[1]))) for table in tables]
    return jnp.asarray(np.concatenate(padded, 0).astype(np.float32))


def y_tables():
    k = np.arange(16)
    theta = 2.0 * np.pi * (np.outer(k, np.array(ORDER_Y)) % 16) / 16
    eyes = np.einsum("hg,qr->hgqr", np.eye(2), np.eye(2))
    table = np.einsum("kjoc,hgqr->jhqcgokr", as_real(theta, False), eyes).reshape(128, 128)
    table_back = np.einsum("kjoc,hgqr->jgrohckq", as_real(theta, True) / 512.0, eyes).reshape(128, 128)
    phi = 2.0 * np.pi * np.outer(np.arange(NV) - 4, k) / 512
    wide = np.broadcast_to(phi[:, None, None, :, None], (NV, 2, 2, 16, 2)).reshape(NV, 128)
    psi = 2.0 * np.pi * (np.outer(np.array(ORDER_X), np.arange(NV) - 4) % 32) / 32
    rows = np.concatenate([np.cos(psi), np.sin(psi)], 1)
    rows_back = np.concatenate([np.cos(psi.T), -np.sin(psi.T)], 1)
    turn = (np.cos(wide), np.sin(wide))
    return in_rows(*turn, table, rows), in_rows(*turn, table_back, rows_back)


def x_tables():
    k0 = np.arange(32)
    alpha = 2.0 * np.pi * (np.outer(k0, np.array(ORDER_X)) % 32) / 32
    rows = np.concatenate([np.cos(alpha), np.sin(alpha)], 1)
    rows_back = np.concatenate([np.cos(alpha.T), -np.sin(alpha.T)], 1) / 512.0
    beta = 2.0 * np.pi * np.outer(k0, np.arange(NU) - 2) / 256
    phi = 2.0 * np.pi * (k0[:, None] + 32 * np.arange(8)[None, :]) / 512
    return in_rows(rows, rows_back, np.concatenate([np.cos(beta), np.sin(beta), np.cos(phi), np.sin(phi)], 1))


def mm(a, b):
    return lax.dot_general(a, b, (((1,), (0,)), ((), ())), preferred_element_type=F32)


def mm_nt(a, b):
    return lax.dot_general(a, b, (((1,), (1,)), ((), ())), preferred_element_type=F32)


def halves(value):
    high = value.astype(BF16)
    return high, (value - high.astype(F32)).astype(BF16)


def thrice(value, axis):
    high, low = halves(value)
    return jnp.concatenate([high, low, high], axis=axis)


def thrice_other(value, axis):
    high, low = halves(value)
    return jnp.concatenate([high, high, low], axis=axis)


def twice(value, axis):
    return jnp.concatenate([value, value], axis=axis)


def iota(shape, axis):
    return lax.broadcasted_iota(jnp.int32, shape, axis)


def turned(value):
    bit = (iota(value.shape, 1) // 32) % 2
    return jnp.where(bit == 0, pltpu.roll(value, 96, 1), -pltpu.roll(value, 32, 1))


def crossed(value):
    half = iota(value.shape, 1) // 64
    return pltpu.roll(value, 64, 1) + jnp.where(half == 0, value, -value)


def layer_picks(anchor):
    fan = jnp.where(iota((TILES, 256), 0) == (iota((TILES, 256), 1) // 8) % TILES, 1.0, 0.0).astype(BF16)
    low = mm(anchor[2:3, :].astype(F32).astype(BF16), fan)
    at = iota((1, 256), 1)
    want = low + ((at // 128) * 64 + ((at // 4) % 2) * 32 + at % 4).astype(F32)
    return jnp.where(iota((128, 256), 0) == want.astype(jnp.int32), 1.0, 0.0).astype(BF16)


def place(anchor_ref, t):
    x = (anchor_ref[0, t] & 15) + 1
    y = (anchor_ref[1, t] & 31) + 1
    starts = (((x + 1) >> 1) * NV + y, (x >> 1) * NV + y)
    return x & 1, starts


def as_row(slot):
    return jnp.concatenate([slot[r : r + 1, :] for r in range(SOURCES // 128)], axis=1)


def slot_picks(slot):
    return jnp.where(iota((SLOTS, SOURCES), 0) == (slot & 127), 1.0, 0.0).astype(BF16)


def side_by_side(ref, n):
    return jnp.concatenate([ref[n], ref[n + 1]], axis=1)


def spread_kernel(
    charges_hbm,
    slot_hbm,
    anchor_hbm,
    pairs_hbm,
    proj_hbm,
    tables_hbm,
    out_ref,
    slots_ref,
    ints_ref,
    charges_ref,
    slot_ref,
    anchor_ref,
    anchor_vec,
    pairs_vec,
    proj_ref,
    tables_ref,
    nodes,
    layers,
    patch,
    cells,
    sems,
):
    fetched = (
        (charges_hbm, charges_ref),
        (slot_hbm, slot_ref),
        (anchor_hbm, anchor_ref),
        (anchor_hbm, anchor_vec),
        (pairs_hbm, pairs_vec),
    ) + tuple((proj_hbm.at[n : n + 8], proj_ref.at[n : n + 8]) for n in range(0, TILES, 8))
    fetched = fetched + ((tables_hbm, tables_ref),)
    copies = [pltpu.make_async_copy(src, dst, sems.at[n]) for n, (src, dst) in enumerate(fetched)]
    for copy in copies:
        copy.start()
    cells[...] = jnp.zeros_like(cells)
    for copy in copies[:5]:
        copy.wait()
    ints_ref[...] = jnp.zeros_like(ints_ref)
    ints_ref[0 : SOURCES // 128, :] = slot_ref[...]
    ints_ref[16:19, 0:TILES] = anchor_vec[...]
    ints_ref[20:22, 0:PAIRS] = pairs_vec[...]
    slot = as_row(slot_ref[...])
    row = iota((32, SOURCES), 0)
    charge = jnp.where(row % 2 == 0, charges_ref[0:1, :], charges_ref[1:2, :])
    held = jnp.where(row // 2 == (slot >> 7), charge, 0.0).astype(BF16)
    slots_ref[...] = mm_nt(held, slot_picks(slot))
    picks = layer_picks(anchor_vec[...])
    first = iota((4, SLOTS), 0) < 2
    for t in range(0, TILES, 2):
        if t % 8 == 0:
            copies[5 + t // 8].wait()
        mine = slots_ref[2 * t : 2 * t + 4, :]
        mine = jnp.concatenate([jnp.where(first, mine, 0.0), jnp.where(first, 0.0, mine)], axis=1)
        nodes[2 * t : 2 * t + 4, :] = mm_nt(mine.astype(BF16), side_by_side(proj_ref, t))
    value = nodes[...]
    layer = iota((32, 128), 1) % 4
    for half in range(2):
        for b in range(4):
            part = value[:, 128 * half : 128 * half + 128]
            layers[pl.ds(128 * half + b, 32, stride=4), :] = jnp.where(layer == b, part, 0.0)
    high, low = halves(jnp.concatenate([layers[0:128, :], layers[128:256, :]], axis=1))
    copies[7].wait()
    spread = tables_ref[0:256, :]
    patch[...] = mm(high, spread) + mm(low, spread)
    empty = jnp.zeros((8, 128), F32)
    for t in range(TILES):
        odd, starts = place(anchor_ref, t)
        even_part = patch[8 * t : 8 * t + 8, 0:128]
        odd_part = patch[8 * t : 8 * t + 8, 128:256]
        parts = (jnp.where(odd == 1, odd_part, even_part), jnp.where(odd == 1, even_part, odd_part))
        for h in range(2):
            wide = jnp.concatenate([parts[h], empty], axis=1)
            wide = pltpu.roll(wide, starts[h] & 127, 1)
            lane = pl.multiple_of((starts[h] >> 7) * 128, 128)
            cells[128 * h + 8 * t : 128 * h + 8 * t + 8, pl.ds(lane, 256)] = wide
    phase_high = mm(tables_ref[256:384, 0:128], picks).astype(BF16)
    phase_low = mm(tables_ref[256:384, 128:256], picks).astype(BF16)
    phase = jnp.concatenate([phase_high, phase_high, phase_low], axis=1)
    out = mm(phase, thrice(cells[...], 0))
    out_ref[...] = out.astype(BF16)


def y_kernel(in_ref, table_ref, out_ref, hold):
    data = in_ref[...].astype(F32).T.astype(BF16)
    cos, sin = table_ref[0:NV, :], table_ref[NV : 2 * NV, :]
    table = table_ref[2 * NV : 2 * NV + 128, :]
    high, low = halves(jnp.concatenate([table, turned(table)], axis=1))
    both = mm(twice(data, 1), jnp.concatenate([high, low], axis=0))
    rows = thrice_other(table_ref[2 * NV + 128 : 2 * NV + 160, 0 : 2 * NV], 1)
    for u in range(0, NU, 2):
        lines = []
        for n in (u, u + 1):
            plain = both[NV * n : NV * (n + 1), 0:128]
            turn = both[NV * n : NV * (n + 1), 128:256]
            lines.append(jnp.concatenate([plain * cos + turn * sin, turn * cos - plain * sin], axis=0))
        out = mm(rows, thrice(jnp.concatenate(lines, axis=1), 0))
        hold[pl.ds(u, 32, stride=NU), :] = out[:, 0:128]
        hold[pl.ds(u + 1, 32, stride=NU), :] = out[:, 128:256]
    out_ref[...] = hold[0:ROWS, :].reshape(LINES).astype(BF16)


def rotated(value, cos, sin):
    plain, turn = value
    return plain * cos + turn * sin, turn * cos - plain * sin


def eighths(value, count, sign):
    plain, turn = value
    if count == 0:
        return value
    if count == 2:
        return (turn, -plain) if sign > 0 else (-turn, plain)
    if count == 3:
        return eighths(eighths(value, 2, sign), 1, sign)
    root = math.sqrt(0.5)
    if sign > 0:
        return (plain + turn) * root, (turn - plain) * root
    return (plain - turn) * root, (turn + plain) * root


def short_dft(values, sign):
    count = len(values)
    if count == 1:
        return values
    even, odd = short_dft(values[0::2], sign), short_dft(values[1::2], sign)
    odd = [eighths(value, 8 // count * n, sign) for n, value in enumerate(odd)]
    sums = [(a[0] + b[0], a[1] + b[1]) for a, b in zip(even, odd)]
    return sums + [(a[0] - b[0], a[1] - b[1]) for a, b in zip(even, odd)]


def line_pair(rows, plain, turn):
    four = jnp.concatenate(
        [jnp.concatenate([plain, turn], axis=1), jnp.concatenate([turn, -plain], axis=1)], axis=0
    ).astype(BF16)
    return mm(rows, twice(four, 0))


def x_kernel(in_ref, real_ref, imag_ref, table_ref, out_ref, hold, hold_turned):
    into = jnp.concatenate(halves(table_ref[0:32, 0:64]), axis=1)
    back = thrice_other(table_ref[32:64, 0:64], 1)
    angles = table_ref[64:96, :]
    second = iota((32, 128), 1) >= 64

    def step(u):
        shape = (32, 128)
        cos, sin = angles[:, u : u + 1], angles[:, NU + u : NU + u + 1]
        return jnp.broadcast_to(cos, shape), jnp.broadcast_to(sin, shape)

    def fold(n):
        n = n + 2 * NU
        return jnp.where(second, angles[:, n : n + 1], 1.0), jnp.where(second, angles[:, n + 8 : n + 9], 0.0)

    data = in_ref[...].astype(F32).reshape(ROWS, 128)
    hold[0:ROWS, :] = data
    hold_turned[0:ROWS, :] = turned(data)
    classes = [None] * 8
    for u in range(NU):
        plain = hold[pl.ds(u, 32, stride=NU), :]
        both = line_pair(into, plain, hold_turned[pl.ds(u, 32, stride=NU), :])
        value = rotated((both[:, 0:128], both[:, 128:256]), *step(u))
        at = (u - 2) % 8
        classes[at] = value if classes[at] is None else tuple(a + b for a, b in zip(classes[at], value))
    lines = short_dft(classes, 1)

    def wide(green):
        green = green.reshape(32, 512)
        first, second = green[:, 0:256], green[:, 256:512]
        return jnp.concatenate([first, first, second, second], axis=0).T

    real, imag = wide(real_ref[...]), wide(imag_ref[...])
    for n in range(8):
        rows = slice(32 * n, 32 * n + 32)
        cos, sin = fold(n)
        plain, turn = rotated(lines[n], cos, sin)
        plain, turn = crossed(plain), crossed(turn)
        plain, turn = plain * real[rows] - turn * imag[rows], turn * real[rows] + plain * imag[rows]
        lines[n] = rotated((crossed(plain), crossed(turn)), cos, -sin)
    classes = short_dft(lines, -1)
    for u in range(0, NU, 2):
        values = []
        for n in (u, u + 1):
            cos, sin = step(n)
            values.append(jnp.concatenate(rotated(classes[(n - 2) % 8], cos, -sin), axis=0))
        out = mm(back, thrice(jnp.concatenate(values, axis=1), 0))
        hold[pl.ds(u, 32, stride=NU), :] = out[:, 0:128]
        hold[pl.ds(u + 1, 32, stride=NU), :] = out[:, 128:256]
    out_ref[...] = hold[0:ROWS, :].reshape(LINES).astype(BF16)


def y_back_kernel(in_ref, table_ref, out_ref, hold, hold_turned):
    data = in_ref[...].astype(F32).reshape(ROWS, 128)
    hold[0:ROWS, :] = data
    hold_turned[0:ROWS, :] = turned(data)
    cos, sin = table_ref[0:NV, :], table_ref[NV : 2 * NV, :]
    tab = thrice_other(table_ref[2 * NV : 2 * NV + 128, :], 1)
    rows = jnp.concatenate(halves(table_ref[2 * NV + 128 : 3 * NV + 128, 0:64]), axis=1)
    lines = []
    for u in range(NU):
        plain = hold[pl.ds(u, 32, stride=NU), :]
        turn = hold_turned[pl.ds(u, 32, stride=NU), :]
        both = line_pair(rows, plain, turn)
        lines.append(both[:, 0:128] * cos - both[:, 128:256] * sin)
    lines.append(jnp.zeros((CELLS - NU * NV, 128), F32))
    out = mm_nt(tab, thrice(jnp.concatenate(lines, axis=0), 1))
    out_ref[...] = out.astype(BF16)


def node_lanes():
    node = iota((256, 256), 0)
    lane = ((node >> 5) & 1) * 128 + (node >> 6) * NV + ((node >> 2) & 7)
    return jnp.where(iota((256, 256), 1) == lane, 1.0, 0.0).astype(BF16)


def gather_kernel(
    in_ref,
    ints_ref,
    proj_ref,
    slots_ref,
    blocks_ref,
    table_ref,
    out_ref,
    anchor_ref,
    cells,
    patch,
    layers,
    nodes,
    pick,
    near,
    total,
    sem,
):
    copy = pltpu.make_async_copy(ints_ref.at[16:24], anchor_ref, sem)
    copy.start()
    slot = as_row(ints_ref[0 : SOURCES // 128, :])
    pick[...] = slot_picks(slot)
    picks = layer_picks(ints_ref[16:19, 0:TILES])
    tab = halves(table_ref[...])
    phase = mm(jnp.concatenate(tab, axis=0), picks).T.astype(BF16)
    field = mm(phase, twice(in_ref[...], 0))
    cells[...] = field.astype(BF16).astype(F32)
    copy.wait()
    sign = jnp.where(iota((2, 128), 0) == 0, -1.0, 1.0)
    values = []
    for q in range(0, PAIRS, 2):
        lines = []
        for n in (q, q + 1):
            source = slots_ref[pl.ds(anchor_ref[5, n] * 2, 2), :]
            turn = jnp.concatenate([source[1:2], source[0:1]], axis=0) * sign
            lines.append(jnp.concatenate([source, turn], axis=1))
        blocks = jnp.concatenate([side_by_side(blocks_ref.at[q], 0), side_by_side(blocks_ref.at[q + 1], 0)], axis=0)
        value = mm_nt(jnp.concatenate(lines, axis=0).astype(BF16), blocks)
        values.extend((value[0:2, 0:SLOTS], value[2:4, SLOTS:]))
    near[...] = jnp.zeros_like(near)
    for q in range(PAIRS):
        target = pl.ds(anchor_ref[4, q] * 2, 2)
        near[target, :] = near[target, :] + values[q]
    for t in range(TILES):
        odd, starts = place(anchor_ref, t)
        parts = []
        for h in range(2):
            lane = pl.multiple_of((starts[h] >> 7) * 128, 128)
            wide = cells[128 * h + 8 * t : 128 * h + 8 * t + 8, pl.ds(lane, 256)]
            parts.append(pltpu.roll(wide, (256 - (starts[h] & 127)) & 255, 1)[:, 0:128])
        patch[8 * t : 8 * t + 8, 0:128] = jnp.where(odd == 1, parts[1], parts[0])
        patch[8 * t : 8 * t + 8, 128:256] = jnp.where(odd == 1, parts[0], parts[1])
    value = mm_nt(patch[...].astype(BF16), node_lanes())
    layers[0:128, :] = value[:, 0:128]
    layers[128:256, :] = value[:, 128:256]
    layer = iota((32, 128), 1) % 4
    for half in range(2):
        value = layers[pl.ds(128 * half, 32, stride=4), :]
        for b in range(1, 4):
            value = jnp.where(layer == b, layers[pl.ds(128 * half + b, 32, stride=4), :], value)
        nodes[:, 128 * half : 128 * half + 128] = value
    first = iota((4, SLOTS), 0) < 2
    for t in range(0, TILES, 2):
        value = mm(nodes[2 * t : 2 * t + 4, :].astype(BF16), side_by_side(proj_ref, t))
        total[2 * t : 2 * t + 4, :] = jnp.where(first, value[:, 0:SLOTS], value[:, SLOTS:])
    value = mm(jnp.concatenate(halves(total[...] + near[...]), axis=1), twice(pick[...], 0))
    value = jnp.where(iota((32, SOURCES), 0) // 2 == (slot >> 7), value, 0.0)
    value = value[0:8] + value[8:16] + value[16:24] + value[24:32]
    value = value + pltpu.roll(value, 4, 0)
    value = value + pltpu.roll(value, 2, 0)
    out_ref[...] = value[0:2]


VM = pl.BlockSpec(memory_space=pltpu.VMEM)
HB = pl.BlockSpec(memory_space=pltpu.HBM)


def call(kernel, outs, in_specs, scratch, flops, moved):
    return pl.pallas_call(
        kernel,
        out_shape=outs,
        in_specs=in_specs,
        out_specs=[VM] * len(outs),
        scratch_shapes=scratch,
        compiler_params=pltpu.CompilerParams(vmem_limit_bytes=VMEM_LIMIT),
        cost_estimate=pl.CostEstimate(flops=flops, bytes_accessed=moved, transcendentals=0),
    )


def shape(*dims, dtype=F32):
    return jax.ShapeDtypeStruct(dims, dtype)


def held(*dims, dtype=F32):
    return pltpu.VMEM(dims, dtype)


def swap(cells, axis):
    parts = lax.axis_size(axis)
    blocks = cells.reshape((parts, -1) + cells.shape[1:] if cells.ndim == 3 else (parts, 8, -1))
    order = ORDER_X if axis == "gx" else ORDER_Y
    moved = lax.all_to_all(blocks, axis, 0, 0, axis_index_groups=[list(order)], tiled=True)
    return moved.reshape(cells.shape)


def body(charges, source_slot, tile_anchor, projection, near_pairs, near_blocks, green_real, green_imag):
    first, z_back = z_tables()
    y_table, y_back = y_tables()
    block = pltpu.VMEM((ROWS + 16, 128), F32)
    cells, slots, ints = call(
        spread_kernel,
        [held(128, CELLS, dtype=BF16), held(32, SLOTS), held(24, 128, dtype=jnp.int32)],
        [HB] * 6,
        [
            pltpu.VMEM((2, SOURCES), F32),
            pltpu.VMEM((SOURCES // 128, 128), jnp.int32),
            pltpu.SMEM((3, TILES), jnp.int32),
            pltpu.VMEM((3, TILES), jnp.int32),
            pltpu.VMEM((2, PAIRS), jnp.int32),
            pltpu.VMEM((TILES, 256, SLOTS), BF16),
            pltpu.VMEM((384, 256), BF16),
            pltpu.VMEM((32, 256), F32),
            pltpu.VMEM((264, 128), F32),
            pltpu.VMEM((128, 256), F32),
            pltpu.VMEM((256, CELLS), F32),
            pltpu.SemaphoreType.DMA((8,)),
        ],
        10**9,
        2 * 10**6,
    )(
        *[
            pltpu.with_memory_space_constraint(array, pltpu.HBM)
            for array in (charges, source_slot.reshape(-1, 128), tile_anchor.T, near_pairs.T, projection, first)
        ]
    )
    cells = swap(cells, "gy")
    line_shape = held(*LINES, dtype=BF16)
    lines = call(y_kernel, [line_shape], [VM] * 2, [block], 10**9, 10**6)(cells, y_table)[0]
    lines = swap(lines, "gx")
    lines = call(x_kernel, [line_shape], [VM] * 4, [block] * 2, 10**9, 10**6)(
        lines, green_real.transpose(1, 2, 0), green_imag.transpose(1, 2, 0), x_tables()
    )[0]
    lines = swap(lines, "gx")
    cells = call(y_back_kernel, [held(128, CELLS, dtype=BF16)], [VM] * 2, [block] * 2, 10**9, 10**6)(lines, y_back)[0]
    cells = swap(cells, "gy")
    return call(
        gather_kernel,
        [shape(2, SOURCES)],
        [VM] * 6,
        [
            pltpu.SMEM((8, 128), jnp.int32),
            pltpu.VMEM((256, CELLS), F32),
            pltpu.VMEM((128, 256), F32),
            pltpu.VMEM((264, 128), F32),
            pltpu.VMEM((32, 256), F32),
            pltpu.VMEM((SLOTS, SOURCES), BF16),
            pltpu.VMEM((32, SLOTS), F32),
            pltpu.VMEM((32, SLOTS), F32),
            pltpu.SemaphoreType.DMA,
        ],
        10**9,
        2 * 10**6,
    )(cells, ints, projection, slots, near_blocks, z_back)[0]


def solution(mesh):
    return jax.shard_map(
        body,
        mesh=mesh,
        in_specs=(
            P(None, ("gx", "gy")),
            P(("gx", "gy")),
            P(("gx", "gy"), None),
            P(("gx", "gy"), None, None),
            P(("gx", "gy"), None),
            P(("gx", "gy"), None, None, None),
            P(None, "gx", "gy"),
            P(None, "gx", "gy"),
        ),
        out_specs=P(None, ("gx", "gy")),
        check_vma=False,
    )
```

```python
import math

import jax
import jax.numpy as jnp
import ml_dtypes
import numpy as np
from jax import lax
from jax.experimental import pallas as pl
from jax.experimental.pallas import tpu as pltpu
from jax.sharding import PartitionSpec as P

TILES = 16
SLOTS = 128
PAIRS = 8
SOURCES = 1536
NU = 12
LINES = (96, 4, 128)
ROWS = 384
ORDER_X = (24, 27, 4, 12, 25, 10, 26, 19, 28, 1, 11, 6, 17, 14, 23, 16, 13, 20, 0, 5, 30, 8, 2, 21, 31, 29, 3, 22, 7, 15, 9, 18)
ORDER_Y = tuple(2 * z + x for x in range(2) for z in range(8))
NV = 40
CELLS = 512
F32 = jnp.float32
BF16 = jnp.bfloat16
VMEM_LIMIT = 16 * 1024 * 1024


def split_table(table):
    high = table.astype(np.float32).astype(ml_dtypes.bfloat16)
    low = (table - high.astype(np.float64)).astype(np.float32).astype(ml_dtypes.bfloat16)
    return high, low


def as_real(theta, inverse):
    sign = -1.0 if inverse else 1.0
    cos, sin = np.cos(theta), sign * np.sin(theta)
    return np.stack([np.stack([cos, sin], -1), np.stack([-sin, cos], -1)], -2)


def z_tables():
    kz = np.arange(32)
    theta = 2.0 * np.pi * (np.outer(kz, kz) % 32) / 32
    forward = as_real(theta, False).reshape(16, 2, 32, 2, 2)[list(ORDER_Y)]
    table = np.einsum("jqzoc,hg->jhqogcz", forward, np.eye(2)).reshape(128, 128)
    backward = as_real(theta, True).reshape(16, 2, 32, 2, 2)[list(ORDER_Y)] / 32.0
    table_back = np.einsum("jqzoc,hg->jhqcgoz", backward, np.eye(2)).reshape(128, 128)
    first = np.zeros((384, 256), ml_dtypes.bfloat16)
    p = np.arange(256)
    first[p, (p // 32 % 2) * 128 + (p // 64) * NV + p // 4 % 8] = 1.0
    first[256:384, 0:128], first[256:384, 128:256] = split_table(table)
    return jnp.asarray(first), in_rows(table_back)


def in_rows(*tables):
    padded = [np.pad(table, ((0, 0), (0, 128 - table.shape[1]))) for table in tables]
    return jnp.asarray(np.concatenate(padded, 0).astype(np.float32))


def y_tables():
    k = np.arange(16)
    theta = 2.0 * np.pi * (np.outer(k, np.array(ORDER_Y)) % 16) / 16
    eyes = np.einsum("hg,qr->hgqr", np.eye(2), np.eye(2))
    table = np.einsum("kjoc,hgqr->jhqcgokr", as_real(theta, False), eyes).reshape(128, 128)
    table_back = np.einsum("kjoc,hgqr->jgrohckq", as_real(theta, True) / 512.0, eyes).reshape(128, 128)
    phi = 2.0 * np.pi * np.outer(np.arange(NV) - 4, k) / 512
    wide = np.broadcast_to(phi[:, None, None, :, None], (NV, 2, 2, 16, 2)).reshape(NV, 128)
    psi = 2.0 * np.pi * (np.outer(np.array(ORDER_X), np.arange(NV) - 4) % 32) / 32
    rows = np.concatenate([np.cos(psi), np.sin(psi)], 1)
    rows_back = np.concatenate([np.cos(psi.T), -np.sin(psi.T)], 1)
    turn = (np.cos(wide), np.sin(wide))
    return in_rows(*turn, table, rows), in_rows(*turn, table_back, rows_back)


def x_tables():
    k0 = np.arange(32)
    alpha = 2.0 * np.pi * (np.outer(k0, np.array(ORDER_X)) % 32) / 32
    rows = np.concatenate([np.cos(alpha), np.sin(alpha)], 1)
    rows_back = np.concatenate([np.cos(alpha.T), -np.sin(alpha.T)], 1) / 512.0
    beta = 2.0 * np.pi * np.outer(k0, np.arange(NU) - 2) / 256
    phi = 2.0 * np.pi * (k0[:, None] + 32 * np.arange(8)[None, :]) / 512
    return in_rows(rows, rows_back, np.concatenate([np.cos(beta), np.sin(beta), np.cos(phi), np.sin(phi)], 1))


def mm(a, b):
    return lax.dot_general(a, b, (((1,), (0,)), ((), ())), preferred_element_type=F32)


def mm_nt(a, b):
    return lax.dot_general(a, b, (((1,), (1,)), ((), ())), preferred_element_type=F32)


def halves(value):
    high = value.astype(BF16)
    return high, (value - high.astype(F32)).astype(BF16)


def thrice(value, axis):
    high, low = halves(value)
    return jnp.concatenate([high, low, high], axis=axis)


def thrice_other(value, axis):
    high, low = halves(value)
    return jnp.concatenate([high, high, low], axis=axis)


def twice(value, axis):
    return jnp.concatenate([value, value], axis=axis)


def iota(shape, axis):
    return lax.broadcasted_iota(jnp.int32, shape, axis)


def turned(value):
    bit = (iota(value.shape, 1) // 32) % 2
    return jnp.where(bit == 0, pltpu.roll(value, 96, 1), -pltpu.roll(value, 32, 1))


def crossed(value):
    half = iota(value.shape, 1) // 64
    return pltpu.roll(value, 64, 1) + jnp.where(half == 0, value, -value)


def layer_picks(anchor):
    fan = jnp.where(iota((TILES, 256), 0) == (iota((TILES, 256), 1) // 8) % TILES, 1.0, 0.0).astype(BF16)
    low = mm(anchor[2:3, :].astype(F32).astype(BF16), fan)
    at = iota((1, 256), 1)
    want = low + ((at // 128) * 64 + ((at // 4) % 2) * 32 + at % 4).astype(F32)
    return jnp.where(iota((128, 256), 0) == want.astype(jnp.int32), 1.0, 0.0).astype(BF16)


def place(anchor_ref, t):
    x = (anchor_ref[0, t] & 15) + 1
    y = (anchor_ref[1, t] & 31) + 1
    starts = (((x + 1) >> 1) * NV + y, (x >> 1) * NV + y)
    return x & 1, starts


def as_row(slot):
    return jnp.concatenate([slot[r : r + 1, :] for r in range(SOURCES // 128)], axis=1)


def slot_picks(slot):
    return jnp.where(iota((SLOTS, SOURCES), 0) == (slot & 127), 1.0, 0.0).astype(BF16)


def side_by_side(ref, n):
    return jnp.concatenate([ref[n], ref[n + 1]], axis=1)


def spread_kernel(
    charges_hbm,
    slot_hbm,
    anchor_hbm,
    pairs_hbm,
    proj_hbm,
    tables_hbm,
    out_ref,
    slots_ref,
    ints_ref,
    charges_ref,
    slot_ref,
    anchor_ref,
    anchor_vec,
    pairs_vec,
    proj_ref,
    tables_ref,
    nodes,
    layers,
    patch,
    cells,
    sems,
):
    fetched = (
        (charges_hbm, charges_ref),
        (slot_hbm, slot_ref),
        (anchor_hbm, anchor_ref),
        (anchor_hbm, anchor_vec),
        (pairs_hbm, pairs_vec),
    ) + tuple((proj_hbm.at[n : n + 8], proj_ref.at[n : n + 8]) for n in range(0, TILES, 8))
    fetched = fetched + ((tables_hbm, tables_ref),)
    copies = [pltpu.make_async_copy(src, dst, sems.at[n]) for n, (src, dst) in enumerate(fetched)]
    for copy in copies:
        copy.start()
    cells[...] = jnp.zeros_like(cells)
    for copy in copies[:5]:
        copy.wait()
    ints_ref[...] = jnp.zeros_like(ints_ref)
    ints_ref[0 : SOURCES // 128, :] = slot_ref[...]
    ints_ref[16:19, 0:TILES] = anchor_vec[...]
    ints_ref[20:22, 0:PAIRS] = pairs_vec[...]
    slot = as_row(slot_ref[...])
    row = iota((32, SOURCES), 0)
    charge = jnp.where(row % 2 == 0, charges_ref[0:1, :], charges_ref[1:2, :])
    held = jnp.where(row // 2 == (slot >> 7), charge, 0.0).astype(BF16)
    slots_ref[...] = mm_nt(held, slot_picks(slot))
    picks = layer_picks(anchor_vec[...])
    first = iota((4, SLOTS), 0) < 2
    for t in range(0, TILES, 2):
        if t % 8 == 0:
            copies[5 + t // 8].wait()
        mine = slots_ref[2 * t : 2 * t + 4, :]
        mine = jnp.concatenate([jnp.where(first, mine, 0.0), jnp.where(first, 0.0, mine)], axis=1)
        nodes[2 * t : 2 * t + 4, :] = mm_nt(mine.astype(BF16), side_by_side(proj_ref, t))
    value = nodes[...]
    layer = iota((32, 128), 1) % 4
    for half in range(2):
        for b in range(4):
            part = value[:, 128 * half : 128 * half + 128]
            layers[pl.ds(128 * half + b, 32, stride=4), :] = jnp.where(layer == b, part, 0.0)
    high, low = halves(jnp.concatenate([layers[0:128, :], layers[128:256, :]], axis=1))
    copies[7].wait()
    spread = tables_ref[0:256, :]
    patch[...] = mm(high, spread) + mm(low, spread)
    empty = jnp.zeros((8, 128), F32)
    for t in range(TILES):
        odd, starts = place(anchor_ref, t)
        even_part = patch[8 * t : 8 * t + 8, 0:128]
        odd_part = patch[8 * t : 8 * t + 8, 128:256]
        parts = (jnp.where(odd == 1, odd_part, even_part), jnp.where(odd == 1, even_part, odd_part))
        for h in range(2):
            wide = jnp.concatenate([parts[h], empty], axis=1)
            wide = pltpu.roll(wide, starts[h] & 127, 1)
            lane = pl.multiple_of((starts[h] >> 7) * 128, 128)
            cells[128 * h + 8 * t : 128 * h + 8 * t + 8, pl.ds(lane, 256)] = wide
    phase_high = mm(tables_ref[256:384, 0:128], picks).astype(BF16)
    phase_low = mm(tables_ref[256:384, 128:256], picks).astype(BF16)
    phase = jnp.concatenate([phase_high, phase_high, phase_low], axis=1)
    out = mm(phase, thrice(cells[...], 0))
    out_ref[...] = out.astype(BF16)


def y_kernel(in_ref, table_ref, out_ref, hold):
    data = in_ref[...].astype(F32).T.astype(BF16)
    cos, sin = table_ref[0:NV, :], table_ref[NV : 2 * NV, :]
    table = table_ref[2 * NV : 2 * NV + 128, :]
    high, low = halves(jnp.concatenate([table, turned(table)], axis=1))
    both = mm(twice(data, 1), jnp.concatenate([high, low], axis=0))
    rows = thrice_other(table_ref[2 * NV + 128 : 2 * NV + 160, 0 : 2 * NV], 1)
    for u in range(0, NU, 2):
        lines = []
        for n in (u, u + 1):
            plain = both[NV * n : NV * (n + 1), 0:128]
            turn = both[NV * n : NV * (n + 1), 128:256]
            lines.append(jnp.concatenate([plain * cos + turn * sin, turn * cos - plain * sin], axis=0))
        out = mm(rows, thrice(jnp.concatenate(lines, axis=1), 0))
        hold[pl.ds(u, 32, stride=NU), :] = out[:, 0:128]
        hold[pl.ds(u + 1, 32, stride=NU), :] = out[:, 128:256]
    out_ref[...] = hold[0:ROWS, :].reshape(LINES).astype(BF16)


def rotated(value, cos, sin):
    plain, turn = value
    return plain * cos + turn * sin, turn * cos - plain * sin


def eighths(value, count, sign):
    plain, turn = value
    if count == 0:
        return value
    if count == 2:
        return (turn, -plain) if sign > 0 else (-turn, plain)
    if count == 3:
        return eighths(eighths(value, 2, sign), 1, sign)
    root = math.sqrt(0.5)
    if sign > 0:
        return (plain + turn) * root, (turn - plain) * root
    return (plain - turn) * root, (turn + plain) * root


def short_dft(values, sign):
    count = len(values)
    if count == 1:
        return values
    even, odd = short_dft(values[0::2], sign), short_dft(values[1::2], sign)
    odd = [eighths(value, 8 // count * n, sign) for n, value in enumerate(odd)]
    sums = [(a[0] + b[0], a[1] + b[1]) for a, b in zip(even, odd)]
    return sums + [(a[0] - b[0], a[1] - b[1]) for a, b in zip(even, odd)]


def line_pair(rows, plain, turn):
    four = jnp.concatenate(
        [jnp.concatenate([plain, turn], axis=1), jnp.concatenate([turn, -plain], axis=1)], axis=0
    ).astype(BF16)
    return mm(rows, twice(four, 0))


def x_kernel(in_ref, real_ref, imag_ref, table_ref, out_ref, hold, hold_turned):
    into = jnp.concatenate(halves(table_ref[0:32, 0:64]), axis=1)
    back = thrice_other(table_ref[32:64, 0:64], 1)
    angles = table_ref[64:96, :]
    second = iota((32, 128), 1) >= 64

    def step(u):
        shape = (32, 128)
        cos, sin = angles[:, u : u + 1], angles[:, NU + u : NU + u + 1]
        return jnp.broadcast_to(cos, shape), jnp.broadcast_to(sin, shape)

    def fold(n):
        n = n + 2 * NU
        return jnp.where(second, angles[:, n : n + 1], 1.0), jnp.where(second, angles[:, n + 8 : n + 9], 0.0)

    data = in_ref[...].astype(F32).reshape(ROWS, 128)
    hold[0:ROWS, :] = data
    hold_turned[0:ROWS, :] = turned(data)
    classes = [None] * 8
    for u in range(NU):
        plain = hold[pl.ds(u, 32, stride=NU), :]
        both = line_pair(into, plain, hold_turned[pl.ds(u, 32, stride=NU), :])
        value = rotated((both[:, 0:128], both[:, 128:256]), *step(u))
        at = (u - 2) % 8
        classes[at] = value if classes[at] is None else tuple(a + b for a, b in zip(classes[at], value))
    lines = short_dft(classes, 1)

    def wide(green):
        green = green.reshape(32, 512)
        first, second = green[:, 0:256], green[:, 256:512]
        return jnp.concatenate([first, first, second, second], axis=0).T

    real, imag = wide(real_ref[...]), wide(imag_ref[...])
    for n in range(8):
        rows = slice(32 * n, 32 * n + 32)
        cos, sin = fold(n)
        plain, turn = rotated(lines[n], cos, sin)
        plain, turn = crossed(plain), crossed(turn)
        plain, turn = plain * real[rows] - turn * imag[rows], turn * real[rows] + plain * imag[rows]
        lines[n] = rotated((crossed(plain), crossed(turn)), cos, -sin)
    classes = short_dft(lines, -1)
    for u in range(0, NU, 2):
        values = []
        for n in (u, u + 1):
            cos, sin = step(n)
            values.append(jnp.concatenate(rotated(classes[(n - 2) % 8], cos, -sin), axis=0))
        out = mm(back, thrice(jnp.concatenate(values, axis=1), 0))
        hold[pl.ds(u, 32, stride=NU), :] = out[:, 0:128]
        hold[pl.ds(u + 1, 32, stride=NU), :] = out[:, 128:256]
    out_ref[...] = hold[0:ROWS, :].reshape(LINES).astype(BF16)


def y_back_kernel(in_ref, table_ref, out_ref, hold, hold_turned):
    data = in_ref[...].astype(F32).reshape(ROWS, 128)
    hold[0:ROWS, :] = data
    hold_turned[0:ROWS, :] = turned(data)
    cos, sin = table_ref[0:NV, :], table_ref[NV : 2 * NV, :]
    tab = thrice_other(table_ref[2 * NV : 2 * NV + 128, :], 1)
    rows = jnp.concatenate(halves(table_ref[2 * NV + 128 : 3 * NV + 128, 0:64]), axis=1)
    lines = []
    for u in range(NU):
        plain = hold[pl.ds(u, 32, stride=NU), :]
        turn = hold_turned[pl.ds(u, 32, stride=NU), :]
        both = line_pair(rows, plain, turn)
        lines.append(both[:, 0:128] * cos - both[:, 128:256] * sin)
    lines.append(jnp.zeros((CELLS - NU * NV, 128), F32))
    out = mm_nt(tab, thrice(jnp.concatenate(lines, axis=0), 1))
    out_ref[...] = out.astype(BF16)


def node_lanes():
    node = iota((256, 256), 0)
    lane = ((node >> 5) & 1) * 128 + (node >> 6) * NV + ((node >> 2) & 7)
    return jnp.where(iota((256, 256), 1) == lane, 1.0, 0.0).astype(BF16)


def gather_kernel(
    in_ref,
    ints_ref,
    proj_ref,
    slots_ref,
    blocks_ref,
    table_ref,
    out_ref,
    anchor_ref,
    cells,
    patch,
    layers,
    nodes,
    pick,
    near,
    total,
    sem,
):
    copy = pltpu.make_async_copy(ints_ref.at[16:24], anchor_ref, sem)
    copy.start()
    slot = as_row(ints_ref[0 : SOURCES // 128, :])
    pick[...] = slot_picks(slot)
    picks = layer_picks(ints_ref[16:19, 0:TILES])
    tab = halves(table_ref[...])
    phase = mm(jnp.concatenate(tab, axis=0), picks).T.astype(BF16)
    field = mm(phase, twice(in_ref[...], 0))
    cells[...] = field.astype(BF16).astype(F32)
    copy.wait()
    sign = jnp.where(iota((2, 128), 0) == 0, -1.0, 1.0)
    values = []
    for q in range(0, PAIRS, 2):
        lines = []
        for n in (q, q + 1):
            source = slots_ref[pl.ds(anchor_ref[5, n] * 2, 2), :]
            turn = jnp.concatenate([source[1:2], source[0:1]], axis=0) * sign
            lines.append(jnp.concatenate([source, turn], axis=1))
        blocks = jnp.concatenate([side_by_side(blocks_ref.at[q], 0), side_by_side(blocks_ref.at[q + 1], 0)], axis=0)
        value = mm_nt(jnp.concatenate(lines, axis=0).astype(BF16), blocks)
        values.extend((value[0:2, 0:SLOTS], value[2:4, SLOTS:]))
    near[...] = jnp.zeros_like(near)
    for q in range(PAIRS):
        target = pl.ds(anchor_ref[4, q] * 2, 2)
        near[target, :] = near[target, :] + values[q]
    for t in range(TILES):
        odd, starts = place(anchor_ref, t)
        parts = []
        for h in range(2):
            lane = pl.multiple_of((starts[h] >> 7) * 128, 128)
            wide = cells[128 * h + 8 * t : 128 * h + 8 * t + 8, pl.ds(lane, 256)]
            parts.append(pltpu.roll(wide, (256 - (starts[h] & 127)) & 255, 1)[:, 0:128])
        patch[8 * t : 8 * t + 8, 0:128] = jnp.where(odd == 1, parts[1], parts[0])
        patch[8 * t : 8 * t + 8, 128:256] = jnp.where(odd == 1, parts[0], parts[1])
    value = mm_nt(patch[...].astype(BF16), node_lanes())
    layers[0:128, :] = value[:, 0:128]
    layers[128:256, :] = value[:, 128:256]
    layer = iota((32, 128), 1) % 4
    for half in range(2):
        value = layers[pl.ds(128 * half, 32, stride=4), :]
        for b in range(1, 4):
            value = jnp.where(layer == b, layers[pl.ds(128 * half + b, 32, stride=4), :], value)
        nodes[:, 128 * half : 128 * half + 128] = value
    first = iota((4, SLOTS), 0) < 2
    for t in range(0, TILES, 2):
        value = mm(nodes[2 * t : 2 * t + 4, :].astype(BF16), side_by_side(proj_ref, t))
        total[2 * t : 2 * t + 4, :] = jnp.where(first, value[:, 0:SLOTS], value[:, SLOTS:])
    value = mm(jnp.concatenate(halves(total[...] + near[...]), axis=1), twice(pick[...], 0))
    value = jnp.where(iota((32, SOURCES), 0) // 2 == (slot >> 7), value, 0.0)
    value = value[0:8] + value[8:16] + value[16:24] + value[24:32]
    value = value + pltpu.roll(value, 4, 0)
    value = value + pltpu.roll(value, 2, 0)
    out_ref[...] = value[0:2]


VM = pl.BlockSpec(memory_space=pltpu.VMEM)
HB = pl.BlockSpec(memory_space=pltpu.HBM)


def call(kernel, outs, in_specs, scratch, flops, moved):
    return pl.pallas_call(
        kernel,
        out_shape=outs,
        in_specs=in_specs,
        out_specs=[VM] * len(outs),
        scratch_shapes=scratch,
        compiler_params=pltpu.CompilerParams(vmem_limit_bytes=VMEM_LIMIT),
        cost_estimate=pl.CostEstimate(flops=flops, bytes_accessed=moved, transcendentals=0),
    )


def shape(*dims, dtype=F32):
    return jax.ShapeDtypeStruct(dims, dtype)


def held(*dims, dtype=F32):
    return pltpu.VMEM(dims, dtype)


def swap(cells, axis):
    parts = lax.axis_size(axis)
    blocks = cells.reshape((parts, -1) + cells.shape[1:] if cells.ndim == 3 else (parts, 8, -1))
    order = ORDER_X if axis == "gx" else ORDER_Y
    moved = lax.all_to_all(blocks, axis, 0, 0, axis_index_groups=[list(order)], tiled=True)
    return moved.reshape(cells.shape)


def body(charges, source_slot, tile_anchor, projection, near_pairs, near_blocks, green_real, green_imag):
    first, z_back = z_tables()
    y_table, y_back = y_tables()
    block = pltpu.VMEM((ROWS + 16, 128), F32)
    cells, slots, ints = call(
        spread_kernel,
        [held(128, CELLS, dtype=BF16), held(32, SLOTS), held(24, 128, dtype=jnp.int32)],
        [HB] * 6,
        [
            pltpu.VMEM((2, SOURCES), F32),
            pltpu.VMEM((SOURCES // 128, 128), jnp.int32),
            pltpu.SMEM((3, TILES), jnp.int32),
            pltpu.VMEM((3, TILES), jnp.int32),
            pltpu.VMEM((2, PAIRS), jnp.int32),
            pltpu.VMEM((TILES, 256, SLOTS), BF16),
            pltpu.VMEM((384, 256), BF16),
            pltpu.VMEM((32, 256), F32),
            pltpu.VMEM((264, 128), F32),
            pltpu.VMEM((128, 256), F32),
            pltpu.VMEM((256, CELLS), F32),
            pltpu.SemaphoreType.DMA((8,)),
        ],
        10**9,
        2 * 10**6,
    )(
        *[
            pltpu.with_memory_space_constraint(array, pltpu.HBM)
            for array in (charges, source_slot.reshape(-1, 128), tile_anchor.T, near_pairs.T, projection, first)
        ]
    )
    cells = swap(cells, "gy")
    line_shape = held(*LINES, dtype=BF16)
    lines = call(y_kernel, [line_shape], [VM] * 2, [block], 10**9, 10**6)(cells, y_table)[0]
    lines = swap(lines, "gx")
    lines = call(x_kernel, [line_shape], [VM] * 4, [block] * 2, 10**9, 10**6)(
        lines, green_real.transpose(1, 2, 0), green_imag.transpose(1, 2, 0), x_tables()
    )[0]
    lines = swap(lines, "gx")
    cells = call(y_back_kernel, [held(128, CELLS, dtype=BF16)], [VM] * 2, [block] * 2, 10**9, 10**6)(lines, y_back)[0]
    cells = swap(cells, "gy")
    return call(
        gather_kernel,
        [shape(2, SOURCES)],
        [VM] * 6,
        [
            pltpu.SMEM((8, 128), jnp.int32),
            pltpu.VMEM((256, CELLS), F32),
            pltpu.VMEM((128, 256), F32),
            pltpu.VMEM((264, 128), F32),
            pltpu.VMEM((32, 256), F32),
            pltpu.VMEM((SLOTS, SOURCES), BF16),
            pltpu.VMEM((32, SLOTS), F32),
            pltpu.VMEM((32, SLOTS), F32),
            pltpu.SemaphoreType.DMA,
        ],
        10**9,
        2 * 10**6,
    )(cells, ints, projection, slots, near_blocks, z_back)[0]


def solution(mesh):
    return jax.shard_map(
        body,
        mesh=mesh,
        in_specs=(
            P(None, ("gx", "gy")),
            P(("gx", "gy")),
            P(("gx", "gy"), None),
            P(("gx", "gy"), None, None),
            P(("gx", "gy"), None),
            P(("gx", "gy"), None, None, None),
            P(None, "gx", "gy"),
            P(None, "gx", "gy"),
        ),
        out_specs=P(None, ("gx", "gy")),
        check_vma=False,
    )
```
